512 devices in a mesh: col: 64 (over y, z), row: 8 (over x, core).
Axes of the slice: x: 4, y: 4, z: 16, core: 2. Of those that a mesh axis runs over, the one named last changes fastest.
Arguments:
- ground: bfloat16 [512, 16, 4096], P('col'), may hold values from -0.21875 to 0.21875
- response: bfloat16 [512, 16, 4096], P('col'), may hold values from -6 to 6
- pattern: int32 [512, 16], replicated, may hold values from -1 to 511, as said below
Outputs:
- purified: bfloat16 [512, 16, 4096], P(('col', 'row'))
The draws below stay inside these ranges and needn't reach their ends.
Inputs may be any that keep to these rules, and one draw needn't show every extreme that they name: `pattern`: slots [q * 2, (q + 1) * 2) of block row g list distinct block rows of class q whose column group is within 2 of g's column group, cyclically over 64 groups; live entries come first in each class, the rest are -1; every class of every block row has at least one live entry and some have 2; offsets of 2 occur.
All inputs are finite; a program needn't handle non-finite values.
Results may differ from the reference program's by a relative error of at most 0.017.
Values may be sent and summed in bfloat16 or wider, within the bound.
No kernel may reach another device: no remote copies, remote signals or barrier semaphores. Data moves between devices by JAX's collectives and lax.ppermute only.
A program may use at most 64 MiB of HBM per device.

```python
import jax
import jax.numpy as jnp
from jax import lax

BLK = 64
RB = 1
K8 = 2
REACH = 2
NB = 512
SLOTS = 16
N_COL = 64
N_ROW = 8


def draw_pattern(key, part):
    key = jax.random.fold_in(key, 5)
    pick_key, count_key = jax.random.split(key)
    reach_rows = (2 * REACH + 1) * RB
    group_rows = N_ROW * RB
    scores = jax.random.randint(pick_key, (NB, N_ROW, reach_rows), 0, 1 << 20) * reach_rows
    scores = scores + jnp.arange(reach_rows, dtype=jnp.int32)
    chosen = jnp.argsort(scores, axis=-1)[:, :, :K8].astype(jnp.int32)
    offset_cols = chosen // RB - REACH
    within = chosen % RB
    row_ids = jnp.arange(NB, dtype=jnp.int32)
    home_group = row_ids // group_rows
    class_ids = jnp.arange(N_ROW, dtype=jnp.int32)
    far_group = (home_group[:, None, None] + offset_cols) % N_COL
    target = (far_group * N_ROW + class_ids[None, :, None]) * RB + within
    counts = jax.random.randint(count_key, (NB, N_ROW), 1, K8 + 1)
    filled = (row_ids[:, None] + class_ids[None, :]) % 3 == 0
    counts = jnp.where(filled, K8, counts)
    active = jnp.arange(K8, dtype=jnp.int32)[None, None, :] < counts[:, :, None]
    return jnp.where(active, target, -1).reshape(NB, N_ROW * K8).astype(jnp.int32)


def block_scale(rng, dims, cuts, low, largest):
    factor_of = 1.0
    for dim, blocks in cuts:
        draws = jax.random.uniform(jax.random.fold_in(jax.random.fold_in(rng, 6), dim), (blocks,), jnp.float32, low / len(cuts), largest / len(cuts))
        factor_of = factor_of * jnp.repeat(jnp.exp(draws), dims[dim] // blocks).reshape((-1,) + (1,) * (len(dims) - 1 - dim))
    return factor_of


def centred(rng, dims, scale, limit, pieces=(), held_as=jnp.bfloat16):
    entries = scale * jax.random.normal(rng, dims, jnp.float32)
    if pieces:
        entries = entries * block_scale(rng, dims, pieces, -0.22, 0.18)
    return jnp.clip(entries, -limit, limit).astype(held_as)


def setup_inputs(seed: int = 0) -> dict:
    seeds = jax.random.split(jax.random.key(seed), 4)
    return {
        "ground": centred(seeds[0], (NB, SLOTS, BLK * BLK), (12 * BLK) ** -0.5, 0.21875, ((0, 64),)),
        "response": centred(seeds[1], (NB, SLOTS, BLK * BLK), 1.0, 6.0, ((0, 64),)),
        "pattern": draw_pattern(jax.random.fold_in(seeds[3], 71), 0),
    }


def rounded(values):
    return lax.optimization_barrier(values.astype(jnp.bfloat16)).astype(jnp.float32)


def class_parts(left_rows, row_ids, right, pattern):
    pat_rows = pattern[row_ids]
    active = pat_rows >= 0
    target = jnp.where(active, pat_rows, 0)
    pat_far = pattern[target]
    hit_table = (pat_far[:, :, None, :] == pat_rows[:, None, :, None]) & (pat_far[:, :, None, :] >= 0)
    hit_table = hit_table & (pat_rows[:, None, :, None] >= 0) & active[:, :, None, None]
    slot_ids = jnp.arange(SLOTS, dtype=jnp.int32)
    found_slot = jnp.sum(hit_table.astype(jnp.int32) * slot_ids, axis=-1).astype(jnp.int32)
    present = jnp.any(hit_table, axis=-1)
    picked = right[target[:, :, None], found_slot]
    picked = jnp.where(present[..., None], picked, jnp.zeros((), right.dtype))
    left_blocks = jnp.where(active[..., None], left_rows, jnp.zeros((), left_rows.dtype))
    count = row_ids.shape[0]
    left_float = left_blocks.astype(jnp.float32).reshape(count, N_ROW, K8, BLK, BLK)
    right_float = picked.astype(jnp.float32).reshape(count, N_ROW, K8, SLOTS, BLK, BLK)
    product = jnp.einsum("gnapq,gnajqs->gnjps", left_float, right_float)
    return product.reshape(count, N_ROW, SLOTS, BLK * BLK)


def reference(ground, response, pattern):
    group_rows = N_ROW * RB
    starts = jnp.arange(NB // group_rows, dtype=jnp.int32) * group_rows

    def first_block(row_start):
        row_ids = row_start + jnp.arange(group_rows, dtype=jnp.int32)
        ground_left = lax.dynamic_slice_in_dim(ground, row_start, group_rows, 0)
        response_left = lax.dynamic_slice_in_dim(response, row_start, group_rows, 0)
        mix_parts = class_parts(response_left, row_ids, ground, pattern) + class_parts(ground_left, row_ids, response, pattern)
        sq_parts = class_parts(ground_left, row_ids, ground, pattern)
        return jnp.sum(rounded(mix_parts), axis=1), jnp.sum(rounded(sq_parts), axis=1)

    mixed, square = lax.map(first_block, starts)
    mixed = mixed.reshape(NB, SLOTS, BLK * BLK)
    square = square.reshape(NB, SLOTS, BLK * BLK)
    mixed_b = mixed.astype(jnp.bfloat16)
    square_b = square.astype(jnp.bfloat16)

    def second_block(row_start):
        row_ids = row_start + jnp.arange(group_rows, dtype=jnp.int32)
        ground_left = lax.dynamic_slice_in_dim(ground, row_start, group_rows, 0)
        response_left = lax.dynamic_slice_in_dim(response, row_start, group_rows, 0)
        parts = class_parts(response_left, row_ids, square_b, pattern) + class_parts(ground_left, row_ids, mixed_b, pattern)
        return jnp.sum(rounded(parts), axis=1)

    cubic = lax.map(second_block, starts).reshape(NB, SLOTS, BLK * BLK)
    return (3.0 * mixed - 2.0 * cubic).astype(jnp.bfloat16)
```

```python
import jax
import jax.numpy as jnp
from jax import lax
from jax.experimental import pallas as pl
from jax.experimental.pallas import tpu as pltpu
from jax.sharding import PartitionSpec as P

BLK = 64
K8 = 2
REACH = 2
SLOTS = 16
ROWS = 8
WIDE = SLOTS * 8
TILES = BLK * BLK // 128
HALF = TILES
F32, BF16 = jnp.float32, jnp.bfloat16
VMEM_BYTES = 48 * 1024 * 1024


def call(body, name, out_shape, scratch, in_specs, flops, moved):
    del name
    return pl.pallas_call(
        body,
        out_shape=out_shape,
        in_specs=in_specs,
        out_specs=jax.tree.map(lambda _: pl.BlockSpec(memory_space=pltpu.VMEM), out_shape),
        scratch_shapes=scratch,
        compiler_params=pltpu.CompilerParams(vmem_limit_bytes=VMEM_BYTES),
        cost_estimate=pl.CostEstimate(flops=flops, bytes_accessed=moved, transcendentals=0),
    )


def in_vmem(count):
    return [pl.BlockSpec(memory_space=pltpu.VMEM)] * count


def by_slot(rows_ref, g, turned):
    flat = rows_ref[g]
    for t in range(TILES):
        turned[pl.ds(t * SLOTS, SLOTS), :] = flat[:, t * 128 : (t + 1) * 128].astype(F32)
    return [turned[pl.ds(b, TILES, stride=SLOTS), :].astype(BF16) for b in range(SLOTS)]


def slice_body(r_ref, ground_ref, response_ref, out_ref, turned, tiles, pick):
    r = r_ref[0]
    line = lax.broadcasted_iota(jnp.int32, (128, 256), 0)
    lane = lax.broadcasted_iota(jnp.int32, (128, 256), 1)
    half, col = line // BLK, line % BLK - 8 * r
    home = jnp.where((col >= 0) & (col < 8), half * 128 + col, -1024)
    for b in range(SLOTS):
        at = (b % 2) * 64 + (b // 2) * 8
        pick[pl.ds(b * 128, 128), :] = jnp.where(lane - at == home, 1.0, 0.0).astype(BF16)
    for m, rows_ref in enumerate((ground_ref, response_ref)):

        def step(g, _, m=m, rows_ref=rows_ref):
            parts = by_slot(rows_ref, g, turned)
            at = pl.multiple_of((m * ROWS + g) * TILES, TILES)
            for b in range(SLOTS):
                tiles[pl.ds(at, TILES), b * 128 : (b + 1) * 128] = parts[b]
            return 0

        lax.fori_loop(0, ROWS, step, 0)
    cut = jnp.dot(tiles[...], pick[...], preferred_element_type=F32).astype(BF16)
    for m in range(2):
        for g in range(ROWS):
            at = (m * ROWS + g) * TILES
            out_ref[m, g, 0:HALF, :] = cut[at : at + TILES, 0:128]
            out_ref[m, g, HALF:BLK, :] = cut[at : at + TILES, 128:256]


def left_body(ground_ref, response_ref, out_ref, turned):
    src = lax.broadcasted_iota(jnp.int32, (256, 256), 0)
    dst = lax.broadcasted_iota(jnp.int32, (256, 256), 1)
    two, half, col = src // 128, src // BLK % 2, src % BLK
    want = half * 128 + two * BLK + (col % 2) * HALF + col // 2
    turn = jnp.where(dst == want, 1.0, 0.0).astype(BF16)
    for m, rows_ref in enumerate((response_ref, ground_ref)):

        def step(g, _, m=m, rows_ref=rows_ref):
            parts = by_slot(rows_ref, g, turned)
            pairs = [jnp.concatenate(parts[b : b + 2], axis=1) for b in range(0, SLOTS, 2)]
            both = jnp.dot(jnp.concatenate(pairs, axis=0), turn, preferred_element_type=F32).astype(BF16)
            for i in range(SLOTS // 2):
                piece = both[i * TILES : (i + 1) * TILES]
                out_ref[m, g, 0:HALF, i * 128 : (i + 1) * 128] = piece[:, 0:128]
                out_ref[m, g, HALF:BLK, i * 128 : (i + 1) * 128] = piece[:, 128:256]
            return 0

        lax.fori_loop(0, ROWS, step, 0)


def fill_window(window, pieces):
    for o, piece in enumerate(pieces):
        for m in range(2):

            def step(g, _, o=o, m=m, piece=piece):
                block = piece[m, g]
                window[o * ROWS + g, m, :, 0:128] = block
                window[o * ROWS + g, m, :, 128:256] = jnp.concatenate([block[:, 64:128], block[:, 0:64]], axis=1)
                return 0

            lax.fori_loop(0, ROWS, step, 0)


def rights(window, where_ref, same_ref, other_ref, g):
    stacks = ([], [])
    for a in range(SLOTS):
        i = g * SLOTS + a
        k = where_ref[i]
        same = jnp.broadcast_to(same_ref[pl.ds(i, 1), :], (16, 128)).astype(BF16)
        other = jnp.broadcast_to(other_ref[pl.ds(i, 1), :], (16, 128)).astype(BF16)
        same, other = jnp.concatenate([same] * 4, axis=0), jnp.concatenate([other] * 4, axis=0)
        for m in range(2):
            both = window[k, m]
            stacks[m].append(both[:, 0:128] * same + both[:, 128:256] * other)
    return [jnp.concatenate(stack, axis=0) for stack in stacks]


def first_body(where_ref, same_ref, other_ref, x0, x1, x2, x3, x4, left_ref, pair_ref, mixed_ref, window):
    fill_window(window, (x0, x1, x2, x3, x4))

    def step(g, _):
        ground, response = rights(window, where_ref, same_ref, other_ref, g)
        left_response, left_ground = left_ref[0, g], left_ref[1, g]
        mixed = jnp.dot(left_response, ground, preferred_element_type=F32)
        mixed = mixed + jnp.dot(left_ground, response, preferred_element_type=F32)
        square = jnp.dot(left_ground, ground, preferred_element_type=F32)
        mixed_ref[g] = mixed
        pair_ref[0, g] = square.astype(BF16)
        pair_ref[1, g] = mixed.astype(BF16)
        return 0

    lax.fori_loop(0, ROWS, step, 0)


def second_body(where_ref, same_ref, other_ref, x0, x1, x2, x3, x4, left_ref, mixed_ref, out_ref, window):
    fill_window(window, (x0, x1, x2, x3, x4))

    def step(g, _):
        square, mixed = rights(window, where_ref, same_ref, other_ref, g)
        cubic = jnp.dot(left_ref[0, g], square, preferred_element_type=F32)
        cubic = cubic + jnp.dot(left_ref[1, g], mixed, preferred_element_type=F32)
        out_ref[g] = (3.0 * mixed_ref[g] - 2.0 * cubic).astype(BF16)
        return 0

    lax.fori_loop(0, ROWS, step, 0)


def join_body(in_ref, out_ref, turned):
    chunk = lax.broadcasted_iota(jnp.int32, (TILES, 128), 1) // 8
    parts = [in_ref[i % 8, (i // 8) * HALF : (i // 8 + 1) * HALF, :].astype(F32) for i in range(16)]
    for bit in (1, 2, 4, 8):
        low = chunk // bit % 2 == 0
        for i in range(16):
            if i & bit:
                continue
            a, b = parts[i], parts[i | bit]
            parts[i] = jnp.where(low, a, pltpu.roll(b, 8 * bit, 1))
            parts[i | bit] = jnp.where(low, pltpu.roll(a, 128 - 8 * bit, 1), b)
    for i in range(16):
        j = 2 * (i % 8) + i // 8
        turned[pl.ds(j * TILES, TILES), :] = parts[i]
    for t in range(TILES):
        out_ref[0, :, t * 128 : (t + 1) * 128] = turned[pl.ds(t, SLOTS, stride=TILES), :].astype(BF16)


def from_behind(block, distance):
    size = lax.axis_size("col")
    return lax.ppermute(block, "col", [((i - distance) % size, i) for i in range(size)])


def surround(block):
    back, ahead = from_behind(block, 1), from_behind(block, -1)
    return from_behind(back, 1), back, block, ahead, from_behind(ahead, -1)


def lookups(pattern):
    column = lax.axis_index("col")
    size = lax.axis_size("col")
    mine = lax.dynamic_slice_in_dim(pattern, column * ROWS, ROWS, 0)
    live = mine >= 0
    target = jnp.where(live, mine, 0)
    place = (target // ROWS - column + REACH) % size
    place = jnp.where(live, place, REACH) * ROWS + target % ROWS
    far = pattern[target].reshape(ROWS, SLOTS, ROWS, K8)
    near = mine.reshape(ROWS, 1, ROWS, K8)
    valid = (near >= 0) & live[:, :, None, None]

    def lanes(hit):
        hit = (hit & valid).astype(F32).transpose(0, 1, 3, 2)
        return jnp.broadcast_to(hit[..., None], hit.shape + (8,)).reshape(ROWS * SLOTS, WIDE)

    return place.reshape(-1), lanes(far == near), lanes(far[..., ::-1] == near)


def local(ground, response, pattern):
    rows = jax.ShapeDtypeStruct((2, ROWS, BLK, WIDE), BF16)
    smem = pl.BlockSpec(memory_space=pltpu.SMEM)
    turned = pltpu.VMEM((SLOTS * TILES, 128), F32)
    window = pltpu.VMEM((5 * ROWS, 2, BLK, 2 * WIDE), BF16)
    r = lax.axis_index("row").astype(jnp.int32).reshape(1)
    cut = call(
        slice_body,
        "slice",
        rows,
        [turned, pltpu.VMEM((2 * ROWS * TILES, SLOTS * 128), BF16), pltpu.VMEM((SLOTS * 128, 256), BF16)],
        [smem] + in_vmem(2),
        2 * 512 * 2048 * 256,
        5 << 20,
    )(r, ground, response)
    cut, ground, response, pattern = lax.optimization_barrier((cut, ground, response, pattern))
    pieces = surround(cut)
    left = call(
        left_body,
        "left",
        jax.ShapeDtypeStruct((2, ROWS, BLK, SLOTS * BLK), BF16),
        [turned],
        in_vmem(2),
        2 * 4096 * 256 * 256,
        5 << 20,
    )(ground, response)
    place, same, other = lookups(pattern)
    flops = 2 * ROWS * BLK * 1024 * 128
    pair, mixed = call(
        first_body,
        "first",
        (rows, jax.ShapeDtypeStruct((ROWS, BLK, WIDE), F32)),
        [window],
        [smem] + in_vmem(8),
        3 * flops,
        5 << 20,
    )(place, same, other, *pieces, left)
    pieces = surround(pair)
    part = call(
        second_body,
        "second",
        jax.ShapeDtypeStruct((ROWS, BLK, WIDE), BF16),
        [window],
        [smem] + in_vmem(9),
        2 * flops,
        5 << 20,
    )(place, same, other, *pieces, left, mixed)
    part = lax.all_to_all(part, "row", 0, 0, tiled=True)
    return call(
        join_body,
        "join",
        jax.ShapeDtypeStruct((1, SLOTS, BLK * BLK), BF16),
        [turned],
        in_vmem(1),
        0,
        1 << 18,
    )(part)


def solution(mesh):
    in_specs = (P("col", None, None), P("col", None, None), P())
    out_specs = P(("col", "row"), None, None)
    return jax.shard_map(local, mesh=mesh, in_specs=in_specs, out_specs=out_specs, check_vma=False)
```

```python
import jax
import jax.numpy as jnp
from jax import lax
from jax.experimental import pallas as pl
from jax.experimental.pallas import tpu as pltpu
from jax.sharding import PartitionSpec as P

BLK = 64
K8 = 2
REACH = 2
NB = 512
SLOTS = 16
ROWS = 8
WIDE = SLOTS * 8
TILES = BLK * BLK // 128
HALF = TILES
F32, BF16 = jnp.float32, jnp.bfloat16
PIECES = 2
VMEM_BYTES = 16 * 1024 * 1024


def call(body, name, out_shape, scratch, in_specs, flops, moved):
    del name
    return pl.pallas_call(
        body,
        out_shape=out_shape,
        in_specs=in_specs,
        out_specs=jax.tree.map(lambda _: pl.BlockSpec(memory_space=pltpu.VMEM), out_shape),
        scratch_shapes=scratch,
        compiler_params=pltpu.CompilerParams(vmem_limit_bytes=VMEM_BYTES),
        cost_estimate=pl.CostEstimate(flops=flops, bytes_accessed=moved, transcendentals=0),
    )


def in_vmem(count):
    return [pl.BlockSpec(memory_space=pltpu.VMEM)] * count


def by_slot(rows_ref, g, turned):
    flat = rows_ref[g]
    for t in range(TILES):
        turned[pl.ds(t * SLOTS, SLOTS), :] = flat[:, t * 128 : (t + 1) * 128].astype(F32)
    return [turned[pl.ds(b, TILES, stride=SLOTS), :].astype(BF16) for b in range(SLOTS)]


def exchange(parts):
    parts = list(parts)
    chunk = lax.broadcasted_iota(jnp.int32, parts[0].shape, 1) // 8
    for bit in (1, 2, 4, 8):
        low = chunk // bit % 2 == 0
        for i in range(16):
            if i & bit:
                continue
            a, b = parts[i], parts[i | bit]
            parts[i] = jnp.where(low, a, pltpu.roll(b, 8 * bit, 1))
            parts[i | bit] = jnp.where(low, pltpu.roll(a, 128 - 8 * bit, 1), b)
    return parts


def slice_body(at_ref, ground_hbm, response_hbm, out_ref, held, picked, placed, arrived):
    copies = []
    for m, rows_hbm in enumerate((ground_hbm, response_hbm)):
        for i in range(PIECES):
            part = pl.ds(i * (ROWS // PIECES), ROWS // PIECES)
            copies.append(pltpu.make_async_copy(rows_hbm.at[part], held.at[m, part], arrived.at[m, i]))
    for copy in copies:
        copy.start()
    line = lax.broadcasted_iota(jnp.int32, (1024, 128), 0)
    lane = lax.broadcasted_iota(jnp.int32, (1024, 128), 1)
    col = line % BLK - 8 * at_ref[1]
    pick = jnp.where((col >= 0) & (col < 8) & (lane == line // BLK * 8 + col), 1.0, 0.0).astype(BF16)
    for m in range(2):
        for copy in copies[m * PIECES : (m + 1) * PIECES]:
            copy.wait()
        flat = held[m].reshape(ROWS * SLOTS, BLK * BLK)
        for n in range(4):
            picked[m, n] = jnp.dot(flat[:, n * 1024 : (n + 1) * 1024], pick, preferred_element_type=F32)
            by = [2 * (i % 8) + i // 8 for i in range(16)]
            parts = exchange(picked[m, n, pl.ds(b, ROWS, stride=SLOTS), :] for b in by)
            for i, part in enumerate(parts):
                placed[m, i % 2, pl.ds(n * 8 + i // 2, ROWS, stride=HALF), :] = part
        for half in range(2):
            lines = placed[m, half].astype(BF16).reshape(ROWS, HALF, 128)
            out_ref[m, :, half * HALF : (half + 1) * HALF, :] = lines


def lookup(at_ref, groups_ref, place_ref, same_ref, other_ref):
    column, odd = at_ref[0], at_ref[1] % 2
    groups = groups_ref[...].astype(F32).astype(BF16)
    line = lax.broadcasted_iota(jnp.int32, (NB, WIDE), 0)
    lane = lax.broadcasted_iota(jnp.int32, (NB, WIDE), 1)
    mine = jnp.where(line == column * ROWS + lane // SLOTS, 1.0, 0.0).astype(BF16)
    near = jnp.dot(groups, mine, preferred_element_type=F32)
    slot = lax.broadcasted_iota(jnp.int32, (SLOTS, WIDE), 0)
    pair = lax.broadcasted_iota(jnp.int32, (SLOTS, WIDE), 1)
    home = jnp.sum(jnp.where(slot == pair % SLOTS, near, 0.0), axis=0, keepdims=True)
    live = home >= 0.0
    group = jnp.where(live, home, 0.0).astype(jnp.int32)
    kind = pair[0:1] % SLOTS // K8
    behind = column - group
    size = NB // ROWS
    behind = jnp.where(behind > REACH, behind - size, jnp.where(behind < -REACH, behind + size, behind))
    behind = jnp.where(odd == 1, -behind, behind)
    piece = jnp.where(behind > 0, behind - 1, jnp.where(behind < 0, 1 - behind, 4))
    place_ref[...] = jnp.where(live, piece, 4) * ROWS + kind
    theirs = jnp.where(line == group * ROWS + kind, 1.0, 0.0).astype(BF16)
    far = jnp.dot(groups, theirs, preferred_element_type=F32)
    i = lax.broadcasted_iota(jnp.int32, (SLOTS, SLOTS), 0)
    j = lax.broadcasted_iota(jnp.int32, (SLOTS, SLOTS), 1)
    swap = jnp.where(i // K8 * K8 + 1 - i % K8 == j, 1.0, 0.0).astype(BF16)
    crossed = jnp.dot(swap, far.astype(BF16), preferred_element_type=F32)
    spread = jnp.where(pair // 8 == slot % K8 * ROWS + slot // K8, 1.0, 0.0).astype(BF16)
    for found, out_ref in ((far, same_ref), (crossed, other_ref)):
        hit = jnp.where((found == near) & (near >= 0.0) & live, 1.0, 0.0).astype(BF16)
        out_ref[...] = lax.dot_general(hit, spread, (((0,), (0,)), ((), ())), preferred_element_type=F32)


def left_body(at_ref, groups_ref, ground_ref, response_ref, out_ref, place_ref, same_ref, other_ref, turned):
    lookup(at_ref, groups_ref, place_ref, same_ref, other_ref)
    src = lax.broadcasted_iota(jnp.int32, (256, 256), 0)
    dst = lax.broadcasted_iota(jnp.int32, (256, 256), 1)
    two, half, col = src // 128, src // BLK % 2, src % BLK
    want = half * 128 + two * BLK + (col % 2) * HALF + col // 2
    turn = jnp.where(dst == want, 1.0, 0.0).astype(BF16)
    for m, rows_ref in enumerate((response_ref, ground_ref)):

        def step(g, _, m=m, rows_ref=rows_ref):
            parts = by_slot(rows_ref, g, turned)
            pairs = [jnp.concatenate(parts[b : b + 2], axis=1) for b in range(0, SLOTS, 2)]
            both = jnp.dot(jnp.concatenate(pairs, axis=0), turn, preferred_element_type=F32).astype(BF16)
            for i in range(SLOTS // 2):
                piece = both[i * TILES : (i + 1) * TILES]
                out_ref[g, m * BLK : m * BLK + HALF, i * 128 : (i + 1) * 128] = piece[:, 0:128]
                out_ref[g, m * BLK + HALF : m * BLK + BLK, i * 128 : (i + 1) * 128] = piece[:, 128:256]
            return 0

        lax.fori_loop(0, ROWS, step, 0, unroll=True)


def fill_window(window, pieces):
    for o, piece in enumerate(pieces):
        for m in range(2):
            flat = piece[m].reshape(ROWS * BLK, 128)
            at = o * ROWS * BLK
            window[m, at : at + ROWS * BLK, 0:128] = flat
            window[m, at : at + ROWS * BLK, 128:256] = jnp.concatenate([flat[:, 64:128], flat[:, 0:64]], axis=1)


def rights(window, where_ref, same_ref, other_ref, g):
    stacks = ([], [])
    for a in range(SLOTS):
        i = g * SLOTS + a
        at = pl.multiple_of(where_ref[0, i] * BLK, BLK)
        same = jnp.broadcast_to(same_ref[pl.ds(i, 1), :], (16, 128)).astype(BF16)
        other = jnp.broadcast_to(other_ref[pl.ds(i, 1), :], (16, 128)).astype(BF16)
        same, other = jnp.concatenate([same] * 4, axis=0), jnp.concatenate([other] * 4, axis=0)
        for m in range(2):
            both = window[m, pl.ds(at, BLK), :]
            stacks[m].append(both[:, 0:128] * same + both[:, 128:256] * other)
    return [jnp.concatenate(stack, axis=0) for stack in stacks]


def first_body(where_ref, same_ref, other_ref, x0, x1, x2, x3, x4, left_ref, pair_ref, mixed_ref, window):
    fill_window(window, (x0, x1, x2, x3, x4))

    def step(g, _):
        ground, response = rights(window, where_ref, same_ref, other_ref, g)
        both = jnp.concatenate([ground, response], axis=1)
        product = jnp.dot(left_ref[g], both, preferred_element_type=F32)
        mixed = product[0:BLK, 0:128] + product[BLK:, 128:256]
        mixed_ref[g] = mixed
        pair_ref[0, g] = product[BLK:, 0:128].astype(BF16)
        pair_ref[1, g] = mixed.astype(BF16)
        return 0

    lax.fori_loop(0, ROWS, step, 0, unroll=True)


def second_body(where_ref, same_ref, other_ref, x0, x1, x2, x3, x4, left_ref, mixed_ref, out_ref, window):
    fill_window(window, (x0, x1, x2, x3, x4))

    def step(g, _):
        square, mixed = rights(window, where_ref, same_ref, other_ref, g)
        cubic = jnp.dot(left_ref[g, 0:BLK], square, preferred_element_type=F32)
        cubic = cubic + jnp.dot(left_ref[g, BLK:], mixed, preferred_element_type=F32)
        out_ref[g] = (3.0 * mixed_ref[g] - 2.0 * cubic).astype(BF16)
        return 0

    lax.fori_loop(0, ROWS, step, 0, unroll=True)


def join_body(in_ref, out_ref, turned):
    parts = exchange(in_ref[i % 8, (i // 8) * HALF : (i // 8 + 1) * HALF, :].astype(F32) for i in range(16))
    for i in range(16):
        j = 2 * (i % 8) + i // 8
        turned[pl.ds(j * TILES, TILES), :] = parts[i]
    for t in range(TILES):
        out_ref[0, :, t * 128 : (t + 1) * 128] = turned[pl.ds(t, SLOTS, stride=TILES), :].astype(BF16)


def from_afar(block, distance):
    columns, rows = lax.axis_size("col"), lax.axis_size("row")
    route = []
    for c in range(columns):
        for r in range(rows):
            to = (c + (distance if r % 2 == 0 else -distance)) % columns
            route.append((c * rows + r, to * rows + r))
    return lax.ppermute(block, ("col", "row"), route)


def surround(block):
    return [from_afar(block, distance) for distance in (1, 2, -1, -2)] + [block]


def local(ground, response, pattern):
    rows = jax.ShapeDtypeStruct((2, ROWS, BLK, WIDE), BF16)
    mask = jax.ShapeDtypeStruct((ROWS * SLOTS, WIDE), F32)
    smem = pl.BlockSpec(memory_space=pltpu.SMEM)
    turned = pltpu.VMEM((SLOTS * TILES, 128), F32)
    window = pltpu.VMEM((2, 5 * ROWS * BLK, 2 * WIDE), BF16)
    at = jnp.stack([lax.axis_index("col"), lax.axis_index("row")]).astype(jnp.int32)
    cut = call(
        slice_body,
        "slice",
        rows,
        [
            pltpu.VMEM((2, ROWS, SLOTS, BLK * BLK), BF16),
            pltpu.VMEM((2, 4, ROWS * SLOTS, 128), F32),
            pltpu.VMEM((2, 2, ROWS * HALF, 128), F32),
            pltpu.SemaphoreType.DMA((2, PIECES)),
        ],
        [smem] + [pl.BlockSpec(memory_space=pltpu.HBM)] * 2,
        2 * 1024 * 1024 * 128,
        5 << 20,
    )(at, ground, response)
    cut, ground, response, pattern = lax.optimization_barrier((cut, ground, response, pattern))
    pieces = surround(cut)
    groups = jnp.where(pattern < 0, -1, pattern // ROWS).T
    left, place, same, other = call(
        left_body,
        "left",
        (jax.ShapeDtypeStruct((ROWS, 2 * BLK, SLOTS * BLK), BF16), jax.ShapeDtypeStruct((1, WIDE), jnp.int32), mask, mask),
        [turned],
        [smem] + in_vmem(3),
        2 * 4096 * 256 * 256,
        5 << 20,
    )(at, groups, ground, response)
    flops = 2 * ROWS * BLK * 1024 * 128
    pair, mixed = call(
        first_body,
        "first",
        (rows, jax.ShapeDtypeStruct((ROWS, BLK, WIDE), F32)),
        [window],
        [smem] + in_vmem(8),
        3 * flops,
        5 << 20,
    )(place, same, other, *pieces, left)
    pieces = surround(pair)
    part = call(
        second_body,
        "second",
        jax.ShapeDtypeStruct((ROWS, BLK, WIDE), BF16),
        [window],
        [smem] + in_vmem(9),
        2 * flops,
        5 << 20,
    )(place, same, other, *pieces, left, mixed)
    part = lax.all_to_all(part, "row", 0, 0, tiled=True)
    return call(
        join_body,
        "join",
        jax.ShapeDtypeStruct((1, SLOTS, BLK * BLK), BF16),
        [turned],
        in_vmem(1),
        0,
        1 << 18,
    )(part)


def solution(mesh):
    in_specs = (P("col", None, None), P("col", None, None), P())
    out_specs = P(("col", "row"), None, None)
    return jax.shard_map(local, mesh=mesh, in_specs=in_specs, out_specs=out_specs, check_vma=False)
```

```python
import jax
import jax.numpy as jnp
from jax import lax
from jax.experimental import pallas as pl
from jax.experimental.pallas import tpu as pltpu
from jax.sharding import PartitionSpec as P

BLK = 64
K8 = 2
REACH = 2
NB = 512
SLOTS = 16
ROWS = 8
WIDE = SLOTS * 8
TILES = BLK * BLK // 128
HALF = TILES
F32, BF16 = jnp.float32, jnp.bfloat16
PIECES = 2
VMEM_BYTES = 16 * 1024 * 1024


SLICE_BYTES = int(62.5 * 1024 * 1024)


def call(body, name, out_shape, scratch, in_specs, flops, moved, vmem=VMEM_BYTES):
    del name
    return pl.pallas_call(
        body,
        out_shape=out_shape,
        in_specs=in_specs,
        out_specs=jax.tree.map(lambda _: pl.BlockSpec(memory_space=pltpu.VMEM), out_shape),
        scratch_shapes=scratch,
        compiler_params=pltpu.CompilerParams(vmem_limit_bytes=vmem),
        cost_estimate=pl.CostEstimate(flops=flops, bytes_accessed=moved, transcendentals=0),
    )


def in_vmem(count):
    return [pl.BlockSpec(memory_space=pltpu.VMEM)] * count


def by_slot(rows_ref, g, turned):
    flat = rows_ref[g]
    for t in range(TILES):
        turned[pl.ds(t * SLOTS, SLOTS), :] = flat[:, t * 128 : (t + 1) * 128].astype(F32)
    return [turned[pl.ds(b, TILES, stride=SLOTS), :].astype(BF16) for b in range(SLOTS)]


def exchange(parts):
    parts = list(parts)
    chunk = lax.broadcasted_iota(jnp.int32, parts[0].shape, 1) // 8
    for bit in (1, 2, 4, 8):
        low = chunk // bit % 2 == 0
        for i in range(16):
            if i & bit:
                continue
            a, b = parts[i], parts[i | bit]
            parts[i] = jnp.where(low, a, pltpu.roll(b, 8 * bit, 1))
            parts[i | bit] = jnp.where(low, pltpu.roll(a, 128 - 8 * bit, 1), b)
    return parts


def slice_body(ground_hbm, response_hbm, out_ref, held, picked, placed, arrived):
    copies = []
    for m, rows_hbm in enumerate((ground_hbm, response_hbm)):
        for i in range(PIECES):
            part = pl.ds(i * (ROWS // PIECES), ROWS // PIECES)
            copies.append(pltpu.make_async_copy(rows_hbm.at[part], held.at[m, part], arrived.at[m, i]))
    for copy in copies:
        copy.start()
    line = lax.broadcasted_iota(jnp.int32, (1024, 128), 0)
    lane = lax.broadcasted_iota(jnp.int32, (1024, 128), 1)
    col = line % BLK - 8 * lax.axis_index("row")
    pick = jnp.where((col >= 0) & (col < 8) & (lane == line // BLK * 8 + col), 1.0, 0.0).astype(BF16)
    for m in range(2):
        for copy in copies[m * PIECES : (m + 1) * PIECES]:
            copy.wait()
        flat = held[m].reshape(ROWS * SLOTS, BLK * BLK)
        for n in range(4):
            picked[m, n] = jnp.dot(flat[:, n * 1024 : (n + 1) * 1024], pick, preferred_element_type=F32)
            by = [2 * (i % 8) + i // 8 for i in range(16)]
            parts = exchange(picked[m, n, pl.ds(b, ROWS, stride=SLOTS), :] for b in by)
            for i, part in enumerate(parts):
                placed[m, i % 2, pl.ds(n * 8 + i // 2, ROWS, stride=HALF), :] = part
        for half in range(2):
            lines = placed[m, half].astype(BF16).reshape(ROWS, HALF, 128)
            out_ref[m, :, half * HALF : (half + 1) * HALF, :] = lines


def lookup(groups_ref, place_ref, same_ref, other_ref):
    column, odd = lax.axis_index("col"), lax.axis_index("row") % 2
    groups = groups_ref[...].astype(F32).astype(BF16)
    line = lax.broadcasted_iota(jnp.int32, (NB, WIDE), 0)
    lane = lax.broadcasted_iota(jnp.int32, (NB, WIDE), 1)
    mine = jnp.where(line == column * ROWS + lane // SLOTS, 1.0, 0.0).astype(BF16)
    near = jnp.dot(groups, mine, preferred_element_type=F32)
    slot = lax.broadcasted_iota(jnp.int32, (SLOTS, WIDE), 0)
    pair = lax.broadcasted_iota(jnp.int32, (SLOTS, WIDE), 1)
    home = jnp.sum(jnp.where(slot == pair % SLOTS, near, 0.0), axis=0, keepdims=True)
    live = home >= 0.0
    group = jnp.where(live, home, 0.0).astype(jnp.int32)
    kind = pair[0:1] % SLOTS // K8
    behind = column - group
    size = NB // ROWS
    behind = jnp.where(behind > REACH, behind - size, jnp.where(behind < -REACH, behind + size, behind))
    behind = jnp.where(odd == 1, -behind, behind)
    piece = jnp.where(behind > 0, behind - 1, jnp.where(behind < 0, 1 - behind, 4))
    place_ref[...] = jnp.where(live, piece, 4) * ROWS + kind
    theirs = jnp.where(line == group * ROWS + kind, 1.0, 0.0).astype(BF16)
    far = jnp.dot(groups, theirs, preferred_element_type=F32)
    i = lax.broadcasted_iota(jnp.int32, (SLOTS, SLOTS), 0)
    j = lax.broadcasted_iota(jnp.int32, (SLOTS, SLOTS), 1)
    swap = jnp.where(i // K8 * K8 + 1 - i % K8 == j, 1.0, 0.0).astype(BF16)
    crossed = jnp.dot(swap, far.astype(BF16), preferred_element_type=F32)
    spread = jnp.where(pair // 8 == slot % K8 * ROWS + slot // K8, 1.0, 0.0).astype(BF16)
    for found, out_ref in ((far, same_ref), (crossed, other_ref)):
        hit = jnp.where((found == near) & (near >= 0.0) & live, 1.0, 0.0).astype(BF16)
        out_ref[...] = lax.dot_general(hit, spread, (((0,), (0,)), ((), ())), preferred_element_type=F32)


def left_body(groups_ref, ground_ref, response_ref, out_ref, place_ref, same_ref, other_ref, turned):
    lookup(groups_ref, place_ref, same_ref, other_ref)
    src = lax.broadcasted_iota(jnp.int32, (256, 256), 0)
    dst = lax.broadcasted_iota(jnp.int32, (256, 256), 1)
    two, half, col = src // 128, src // BLK % 2, src % BLK
    want = half * 128 + two * BLK + (col % 2) * HALF + col // 2
    turn = jnp.where(dst == want, 1.0, 0.0).astype(BF16)
    for m, rows_ref in enumerate((response_ref, ground_ref)):

        def step(g, _, m=m, rows_ref=rows_ref):
            parts = by_slot(rows_ref, g, turned)
            pairs = [jnp.concatenate(parts[b : b + 2], axis=1) for b in range(0, SLOTS, 2)]
            both = jnp.dot(jnp.concatenate(pairs, axis=0), turn, preferred_element_type=F32).astype(BF16)
            for i in range(SLOTS // 2):
                piece = both[i * TILES : (i + 1) * TILES]
                out_ref[g, m * BLK : m * BLK + HALF, i * 128 : (i + 1) * 128] = piece[:, 0:128]
                out_ref[g, m * BLK + HALF : m * BLK + BLK, i * 128 : (i + 1) * 128] = piece[:, 128:256]
            return 0

        lax.fori_loop(0, ROWS, step, 0, unroll=True)


def fill_window(window, pieces):
    for o, piece in enumerate(pieces):
        for m in range(2):
            flat = piece[m].reshape(ROWS * BLK, 128)
            at = o * ROWS * BLK
            window[m, at : at + ROWS * BLK, 0:128] = flat
            window[m, at : at + ROWS * BLK, 128:256] = jnp.concatenate([flat[:, 64:128], flat[:, 0:64]], axis=1)


def rights(window, where_ref, same_ref, other_ref, g):
    stacks = ([], [])
    for a in range(SLOTS):
        i = g * SLOTS + a
        at = pl.multiple_of(where_ref[0, i] * BLK, BLK)
        same = jnp.broadcast_to(same_ref[pl.ds(i, 1), :], (16, 128)).astype(BF16)
        other = jnp.broadcast_to(other_ref[pl.ds(i, 1), :], (16, 128)).astype(BF16)
        same, other = jnp.concatenate([same] * 4, axis=0), jnp.concatenate([other] * 4, axis=0)
        for m in range(2):
            both = window[m, pl.ds(at, BLK), :]
            stacks[m].append(both[:, 0:128] * same + both[:, 128:256] * other)
    return [jnp.concatenate(stack, axis=0) for stack in stacks]


def first_body(where_ref, same_ref, other_ref, x0, x1, x2, x3, x4, left_ref, pair_ref, mixed_ref, window):
    fill_window(window, (x0, x1, x2, x3, x4))

    def step(g, _):
        ground, response = rights(window, where_ref, same_ref, other_ref, g)
        both = jnp.concatenate([ground, response], axis=1)
        product = jnp.dot(left_ref[g], both, preferred_element_type=F32)
        mixed = product[0:BLK, 0:128] + product[BLK:, 128:256]
        mixed_ref[g] = mixed
        pair_ref[0, g] = product[BLK:, 0:128].astype(BF16)
        pair_ref[1, g] = mixed.astype(BF16)
        return 0

    lax.fori_loop(0, ROWS, step, 0, unroll=True)


def second_body(where_ref, same_ref, other_ref, x0, x1, x2, x3, x4, left_ref, mixed_ref, out_ref, window):
    fill_window(window, (x0, x1, x2, x3, x4))

    def step(g, _):
        square, mixed = rights(window, where_ref, same_ref, other_ref, g)
        cubic = jnp.dot(left_ref[g, 0:BLK], square, preferred_element_type=F32)
        cubic = cubic + jnp.dot(left_ref[g, BLK:], mixed, preferred_element_type=F32)
        out_ref[g] = (3.0 * mixed_ref[g] - 2.0 * cubic).astype(BF16)
        return 0

    lax.fori_loop(0, ROWS, step, 0, unroll=True)


def join_body(in_ref, out_ref, turned):
    parts = exchange(in_ref[i % 8, (i // 8) * HALF : (i // 8 + 1) * HALF, :].astype(F32) for i in range(16))
    for i in range(16):
        j = 2 * (i % 8) + i // 8
        turned[pl.ds(j * TILES, TILES), :] = parts[i]
    for t in range(TILES):
        out_ref[0, :, t * 128 : (t + 1) * 128] = turned[pl.ds(t, SLOTS, stride=TILES), :].astype(BF16)


def from_afar(block, distance):
    columns, rows = lax.axis_size("col"), lax.axis_size("row")
    route = []
    for c in range(columns):
        for r in range(rows):
            to = (c + (distance if r % 2 == 0 else -distance)) % columns
            route.append((c * rows + r, to * rows + r))
    return lax.ppermute(block, ("col", "row"), route)


def surround(block):
    return [from_afar(block, distance) for distance in (1, 2, -1, -2)] + [block]


def local(ground, response, pattern):
    rows = jax.ShapeDtypeStruct((2, ROWS, BLK, WIDE), BF16)
    mask = jax.ShapeDtypeStruct((ROWS * SLOTS, WIDE), F32)
    smem = pl.BlockSpec(memory_space=pltpu.SMEM)
    turned = pltpu.VMEM((SLOTS * TILES, 128), F32)
    window = pltpu.VMEM((2, 5 * ROWS * BLK, 2 * WIDE), BF16)
    cut = call(
        slice_body,
        "slice",
        rows,
        [
            pltpu.VMEM((2, ROWS, SLOTS, BLK * BLK), BF16),
            pltpu.VMEM((2, 4, ROWS * SLOTS, 128), F32),
            pltpu.VMEM((2, 2, ROWS * HALF, 128), F32),
            pltpu.SemaphoreType.DMA((2, PIECES)),
        ],
        [pl.BlockSpec(memory_space=pltpu.HBM)] * 2,
        2 * 1024 * 1024 * 128,
        5 << 20,
        SLICE_BYTES,
    )(ground, response)
    cut, ground, response, pattern = lax.optimization_barrier((cut, ground, response, pattern))
    pieces = surround(cut)
    groups = jnp.where(pattern < 0, -1, pattern // ROWS).T
    left, place, same, other = call(
        left_body,
        "left",
        (jax.ShapeDtypeStruct((ROWS, 2 * BLK, SLOTS * BLK), BF16), jax.ShapeDtypeStruct((1, WIDE), jnp.int32), mask, mask),
        [turned],
        in_vmem(3),
        2 * 4096 * 256 * 256,
        5 << 20,
    )(groups, ground, response)
    flops = 2 * ROWS * BLK * 1024 * 128
    pair, mixed = call(
        first_body,
        "first",
        (rows, jax.ShapeDtypeStruct((ROWS, BLK, WIDE), F32)),
        [window],
        [smem] + in_vmem(8),
        3 * flops,
        5 << 20,
    )(place, same, other, *pieces, left)
    pieces = surround(pair)
    part = call(
        second_body,
        "second",
        jax.ShapeDtypeStruct((ROWS, BLK, WIDE), BF16),
        [window],
        [smem] + in_vmem(9),
        2 * flops,
        5 << 20,
    )(place, same, other, *pieces, left, mixed)
    part = lax.all_to_all(part, "row", 0, 0, tiled=True)
    return call(
        join_body,
        "join",
        jax.ShapeDtypeStruct((1, SLOTS, BLK * BLK), BF16),
        [turned],
        in_vmem(1),
        0,
        1 << 18,
    )(part)


def solution(mesh):
    in_specs = (P("col", None, None), P("col", None, None), P())
    out_specs = P(("col", "row"), None, None)
    return jax.shard_map(local, mesh=mesh, in_specs=in_specs, out_specs=out_specs, check_vma=False)
```

```python
import jax
import jax.numpy as jnp
from jax import lax
from jax.experimental import pallas as pl
from jax.experimental.pallas import tpu as pltpu
from jax.sharding import PartitionSpec as P

BLK = 64
K8 = 2
REACH = 2
NB = 512
SLOTS = 16
ROWS = 8
WIDE = SLOTS * 8
TILES = BLK * BLK // 128
HALF = TILES
F32, BF16 = jnp.float32, jnp.bfloat16
VMEM_BYTES = 16 * 1024 * 1024


SLICE_BYTES = int(63.1 * 1024 * 1024)


def call(body, name, out_shape, scratch, in_specs, flops, moved, vmem=VMEM_BYTES):
    del name
    return pl.pallas_call(
        body,
        out_shape=out_shape,
        in_specs=in_specs,
        out_specs=jax.tree.map(lambda _: pl.BlockSpec(memory_space=pltpu.VMEM), out_shape),
        scratch_shapes=scratch,
        compiler_params=pltpu.CompilerParams(vmem_limit_bytes=vmem),
        cost_estimate=pl.CostEstimate(flops=flops, bytes_accessed=moved, transcendentals=0),
    )


def in_vmem(count):
    return [pl.BlockSpec(memory_space=pltpu.VMEM)] * count


def by_slot(rows_ref, g, turned):
    flat = rows_ref[g]
    for t in range(TILES):
        turned[pl.ds(t * SLOTS, SLOTS), :] = flat[:, t * 128 : (t + 1) * 128].astype(F32)
    return [turned[pl.ds(b, TILES, stride=SLOTS), :].astype(BF16) for b in range(SLOTS)]


def exchange(parts):
    parts = list(parts)
    chunk = lax.broadcasted_iota(jnp.int32, parts[0].shape, 1) // 8
    for bit in (1, 2, 4, 8):
        low = chunk // bit % 2 == 0
        for i in range(16):
            if i & bit:
                continue
            a, b = parts[i], parts[i | bit]
            parts[i] = jnp.where(low, a, pltpu.roll(b, 8 * bit, 1))
            parts[i | bit] = jnp.where(low, pltpu.roll(a, 128 - 8 * bit, 1), b)
    return parts


def slice_body(ground_hbm, response_hbm, out_ref, held, picked, placed, arrived):
    copies = []
    for m, rows_hbm in enumerate((ground_hbm, response_hbm)):
        copies.append(pltpu.make_async_copy(rows_hbm, held.at[m], arrived.at[m]))
    for copy in copies:
        copy.start()
    line = lax.broadcasted_iota(jnp.int32, (1024, 128), 0)
    lane = lax.broadcasted_iota(jnp.int32, (1024, 128), 1)
    col = line % BLK - 8 * lax.axis_index("row")
    pick = jnp.where((col >= 0) & (col < 8) & (lane == line // BLK * 8 + col), 1.0, 0.0).astype(BF16)
    for m in range(2):
        copies[m].wait()
        flat = held[m].reshape(ROWS * SLOTS, BLK * BLK)
        for n in range(4):
            picked[m, n] = jnp.dot(flat[:, n * 1024 : (n + 1) * 1024], pick, preferred_element_type=F32)
            by = [2 * (i % 8) + i // 8 for i in range(16)]
            parts = exchange(picked[m, n, pl.ds(b, ROWS, stride=SLOTS), :] for b in by)
            for i, part in enumerate(parts):
                placed[m, i % 2, pl.ds(n * 8 + i // 2, ROWS, stride=HALF), :] = part
        for half in range(2):
            lines = placed[m, half].astype(BF16).reshape(ROWS, HALF, 128)
            out_ref[m, :, half * HALF : (half + 1) * HALF, :] = lines


def lookup(groups_ref, place_ref, same_ref, other_ref):
    column, odd = lax.axis_index("col"), lax.axis_index("row") % 2
    groups = groups_ref[...].astype(F32).astype(BF16)
    line = lax.broadcasted_iota(jnp.int32, (NB, WIDE), 0)
    lane = lax.broadcasted_iota(jnp.int32, (NB, WIDE), 1)
    mine = jnp.where(line == column * ROWS + lane // SLOTS, 1.0, 0.0).astype(BF16)
    near = jnp.dot(groups, mine, preferred_element_type=F32)
    slot = lax.broadcasted_iota(jnp.int32, (SLOTS, WIDE), 0)
    pair = lax.broadcasted_iota(jnp.int32, (SLOTS, WIDE), 1)
    home = jnp.sum(jnp.where(slot == pair % SLOTS, near, 0.0), axis=0, keepdims=True)
    live = home >= 0.0
    group = jnp.where(live, home, 0.0).astype(jnp.int32)
    kind = pair[0:1] % SLOTS // K8
    behind = column - group
    size = NB // ROWS
    behind = jnp.where(behind > REACH, behind - size, jnp.where(behind < -REACH, behind + size, behind))
    behind = jnp.where(odd == 1, -behind, behind)
    piece = jnp.where(behind > 0, behind - 1, jnp.where(behind < 0, 1 - behind, 4))
    place_ref[...] = jnp.where(live, piece, 4) * ROWS + kind
    theirs = jnp.where(line == group * ROWS + kind, 1.0, 0.0).astype(BF16)
    far = jnp.dot(groups, theirs, preferred_element_type=F32)
    i = lax.broadcasted_iota(jnp.int32, (SLOTS, SLOTS), 0)
    j = lax.broadcasted_iota(jnp.int32, (SLOTS, SLOTS), 1)
    swap = jnp.where(i // K8 * K8 + 1 - i % K8 == j, 1.0, 0.0).astype(BF16)
    spread = jnp.where(pair // 8 == slot % K8 * ROWS + slot // K8, 1.0, 0.0).astype(BF16)
    facing = jnp.dot(swap, near.astype(BF16), preferred_element_type=F32)
    for ours, out_ref in ((near, same_ref), (facing, other_ref)):
        hit = jnp.where((far == ours) & (ours >= 0.0) & live, 1.0, 0.0).astype(BF16)
        mask = lax.dot_general(hit, spread, (((0,), (0,)), ((), ())), preferred_element_type=F32)
        for n in range(ROWS * SLOTS):
            out_ref[n] = jnp.broadcast_to(mask[n : n + 1], (16, WIDE)).astype(BF16)


def left_body(groups_ref, ground_ref, response_ref, out_ref, place_ref, same_ref, other_ref, turned):
    lookup(groups_ref, place_ref, same_ref, other_ref)
    src = lax.broadcasted_iota(jnp.int32, (256, 256), 0)
    dst = lax.broadcasted_iota(jnp.int32, (256, 256), 1)
    two, half, col = src // 128, src // BLK % 2, src % BLK
    want = half * 128 + two * BLK + (col % 2) * HALF + col // 2
    turn = jnp.where(dst == want, 1.0, 0.0).astype(BF16)
    for m, rows_ref in enumerate((response_ref, ground_ref)):

        def step(g, _, m=m, rows_ref=rows_ref):
            parts = by_slot(rows_ref, g, turned)
            pairs = [jnp.concatenate(parts[b : b + 2], axis=1) for b in range(0, SLOTS, 2)]
            both = jnp.dot(jnp.concatenate(pairs, axis=0), turn, preferred_element_type=F32).astype(BF16)
            for i in range(SLOTS // 2):
                piece = both[i * TILES : (i + 1) * TILES]
                out_ref[g, m * BLK : m * BLK + HALF, i * 128 : (i + 1) * 128] = piece[:, 0:128]
                out_ref[g, m * BLK + HALF : m * BLK + BLK, i * 128 : (i + 1) * 128] = piece[:, 128:256]
            return 0

        lax.fori_loop(0, ROWS, step, 0, unroll=True)


def fill_window(window, pieces):
    for o, piece in enumerate(pieces):
        for m in range(2):
            at = o * ROWS * BLK
            window[m, at : at + ROWS * BLK, :] = piece[m].reshape(ROWS * BLK, WIDE)


def rights(window, where_ref, same_ref, other_ref, g):
    stacks = ([], [])
    for a in range(SLOTS):
        i = g * SLOTS + a
        at = pl.multiple_of(where_ref[0, i] * BLK, BLK)
        same = jnp.concatenate([same_ref[i]] * 4, axis=0)
        other = jnp.concatenate([other_ref[i]] * 4, axis=0)
        for m in range(2):
            blocks = window[m, pl.ds(at, BLK), :]
            stacks[m].append(jnp.concatenate([blocks * same, blocks * other], axis=1))
    return [jnp.concatenate(stack, axis=0) for stack in stacks]


def settle(product):
    return product[:, 0:WIDE] + pltpu.roll(product[:, WIDE:], WIDE // 2, 1)


def first_body(where_ref, same_ref, other_ref, x0, x1, x2, x3, x4, left_ref, pair_ref, mixed_ref, window):
    fill_window(window, (x0, x1, x2, x3, x4))

    def step(g, _):
        ground, response = rights(window, where_ref, same_ref, other_ref, g)
        product = jnp.dot(left_ref[g], ground, preferred_element_type=F32)
        crossed = jnp.dot(left_ref[g, BLK:], response, preferred_element_type=F32)
        mixed = settle(product[0:BLK] + crossed)
        mixed_ref[g] = mixed
        pair_ref[0, g] = settle(product[BLK:]).astype(BF16)
        pair_ref[1, g] = mixed.astype(BF16)
        return 0

    lax.fori_loop(0, ROWS, step, 0, unroll=True)


def second_body(where_ref, same_ref, other_ref, x0, x1, x2, x3, x4, left_ref, mixed_ref, out_ref, window):
    fill_window(window, (x0, x1, x2, x3, x4))

    def step(g, _):
        square, mixed = rights(window, where_ref, same_ref, other_ref, g)
        cubic = jnp.dot(left_ref[g, 0:BLK], square, preferred_element_type=F32)
        cubic = settle(cubic + jnp.dot(left_ref[g, BLK:], mixed, preferred_element_type=F32))
        out_ref[g] = (3.0 * mixed_ref[g] - 2.0 * cubic).astype(BF16)
        return 0

    lax.fori_loop(0, ROWS, step, 0, unroll=True)


def join_body(in_ref, out_ref, turned):
    parts = exchange(in_ref[i % 8, (i // 8) * HALF : (i // 8 + 1) * HALF, :].astype(F32) for i in range(16))
    for i in range(16):
        j = 2 * (i % 8) + i // 8
        turned[pl.ds(j * TILES, TILES), :] = parts[i]
    for t in range(TILES):
        out_ref[0, :, t * 128 : (t + 1) * 128] = turned[pl.ds(t, SLOTS, stride=TILES), :].astype(BF16)


def from_afar(block, distance):
    columns, rows = lax.axis_size("col"), lax.axis_size("row")
    route = []
    for c in range(columns):
        for r in range(rows):
            to = (c + (distance if r % 2 == 0 else -distance)) % columns
            route.append((c * rows + r, to * rows + r))
    return lax.ppermute(block, ("col", "row"), route)


def surround(block):
    return [from_afar(block, distance) for distance in (1, 2, -1, -2)] + [block]


def local(ground, response, pattern):
    rows = jax.ShapeDtypeStruct((2, ROWS, BLK, WIDE), BF16)
    mask = jax.ShapeDtypeStruct((ROWS * SLOTS, 16, WIDE), BF16)
    smem = pl.BlockSpec(memory_space=pltpu.SMEM)
    turned = pltpu.VMEM((SLOTS * TILES, 128), F32)
    window = pltpu.VMEM((2, 5 * ROWS * BLK, WIDE), BF16)
    cut = call(
        slice_body,
        "slice",
        rows,
        [
            pltpu.VMEM((2, ROWS, SLOTS, BLK * BLK), BF16),
            pltpu.VMEM((2, 4, ROWS * SLOTS, 128), F32),
            pltpu.VMEM((2, 2, ROWS * HALF, 128), F32),
            pltpu.SemaphoreType.DMA((2,)),
        ],
        [pl.BlockSpec(memory_space=pltpu.HBM)] * 2,
        2 * 1024 * 1024 * 128,
        5 << 20,
        SLICE_BYTES,
    )(ground, response)
    cut, ground, response, pattern = lax.optimization_barrier((cut, ground, response, pattern))
    pieces = surround(cut)
    groups = jnp.where(pattern < 0, -1, pattern // ROWS).T
    left, place, same, other = call(
        left_body,
        "left",
        (jax.ShapeDtypeStruct((ROWS, 2 * BLK, SLOTS * BLK), BF16), jax.ShapeDtypeStruct((1, WIDE), jnp.int32), mask, mask),
        [turned],
        in_vmem(3),
        2 * 4096 * 256 * 256,
        5 << 20,
    )(groups, ground, response)
    flops = 2 * ROWS * BLK * 1024 * 128
    pair, mixed = call(
        first_body,
        "first",
        (rows, jax.ShapeDtypeStruct((ROWS, BLK, WIDE), F32)),
        [window],
        [smem] + in_vmem(8),
        3 * flops,
        5 << 20,
    )(place, same, other, *pieces, left)
    pieces = surround(pair)
    part = call(
        second_body,
        "second",
        jax.ShapeDtypeStruct((ROWS, BLK, WIDE), BF16),
        [window],
        [smem] + in_vmem(9),
        2 * flops,
        5 << 20,
    )(place, same, other, *pieces, left, mixed)
    part = lax.all_to_all(part, "row", 0, 0, tiled=True)
    return call(
        join_body,
        "join",
        jax.ShapeDtypeStruct((1, SLOTS, BLK * BLK), BF16),
        [turned],
        in_vmem(1),
        0,
        1 << 18,
    )(part)


def solution(mesh):
    in_specs = (P("col", None, None), P("col", None, None), P())
    out_specs = P(("col", "row"), None, None)
    return jax.shard_map(local, mesh=mesh, in_specs=in_specs, out_specs=out_specs, check_vma=False)
```

```python
import jax
import jax.numpy as jnp
from jax import lax
from jax.experimental import pallas as pl
from jax.experimental.pallas import tpu as pltpu
from jax.sharding import PartitionSpec as P

BLK = 64
K8 = 2
REACH = 2
NB = 512
SLOTS = 16
ROWS = 8
WIDE = K8 * BLK
TILES = BLK * BLK // 128
HALF = TILES
F32, BF16 = jnp.float32, jnp.bfloat16
VMEM_BYTES = 16 * 1024 * 1024


SLICE_BYTES = int(63.1 * 1024 * 1024)


def call(body, name, out_shape, scratch, in_specs, flops, moved, vmem=VMEM_BYTES):
    del name
    return pl.pallas_call(
        body,
        out_shape=out_shape,
        in_specs=in_specs,
        out_specs=jax.tree.map(lambda _: pl.BlockSpec(memory_space=pltpu.VMEM), out_shape),
        scratch_shapes=scratch,
        compiler_params=pltpu.CompilerParams(vmem_limit_bytes=vmem),
        cost_estimate=pl.CostEstimate(flops=flops, bytes_accessed=moved, transcendentals=0),
    )


def in_vmem(count):
    return [pl.BlockSpec(memory_space=pltpu.VMEM)] * count


def by_slot(rows_ref, g, turned):
    flat = rows_ref[g]
    for t in range(TILES):
        turned[pl.ds(t * SLOTS, SLOTS), :] = flat[:, t * 128 : (t + 1) * 128].astype(F32)
    return [turned[pl.ds(b, TILES, stride=SLOTS), :].astype(BF16) for b in range(SLOTS)]


def cross(a, b):
    low = lax.broadcasted_iota(jnp.int32, a.shape, 1) < BLK
    return jnp.where(low, a, pltpu.roll(b, BLK, 1)), jnp.where(low, pltpu.roll(a, BLK, 1), b)


def slice_body(ground_hbm, response_hbm, out_ref, held, placed, arrived):
    copies = []
    for m, rows_hbm in enumerate((ground_hbm, response_hbm)):
        copies.append(pltpu.make_async_copy(rows_hbm, held.at[m], arrived.at[m]))
    for copy in copies:
        copy.start()
    line = lax.broadcasted_iota(jnp.int32, (K8 * ROWS, ROWS * SLOTS), 0)
    slot = lax.broadcasted_iota(jnp.int32, (K8 * ROWS, ROWS * SLOTS), 1)
    want = line % ROWS * SLOTS + K8 * lax.axis_index("row") + line // ROWS
    pick = jnp.where(slot == want, 1.0, 0.0).astype(BF16)
    for m in range(2):
        copies[m].wait()
        flat = held[m].reshape(ROWS * SLOTS, BLK * BLK)
        mine = jnp.dot(pick, flat, preferred_element_type=F32)
        for t in range(TILES):
            part = mine[:, t * 128 : (t + 1) * 128]
            for half, lines in enumerate(cross(part[0:ROWS], part[ROWS:])):
                placed[m, half, pl.ds(t, ROWS, stride=HALF), :] = lines
        for half in range(2):
            lines = placed[m, half].astype(BF16).reshape(ROWS, HALF, 128)
            out_ref[m, :, half * HALF : (half + 1) * HALF, :] = lines


def lookup(groups_ref, place_ref, same_ref, other_ref):
    column, odd = lax.axis_index("col"), lax.axis_index("row") % 2
    groups = groups_ref[...].astype(F32).astype(BF16)
    line = lax.broadcasted_iota(jnp.int32, (NB, WIDE), 0)
    lane = lax.broadcasted_iota(jnp.int32, (NB, WIDE), 1)
    mine = jnp.where(line == column * ROWS + lane // SLOTS, 1.0, 0.0).astype(BF16)
    near = jnp.dot(groups, mine, preferred_element_type=F32)
    slot = lax.broadcasted_iota(jnp.int32, (SLOTS, WIDE), 0)
    pair = lax.broadcasted_iota(jnp.int32, (SLOTS, WIDE), 1)
    home = jnp.sum(jnp.where(slot == pair % SLOTS, near, 0.0), axis=0, keepdims=True)
    live = home >= 0.0
    group = jnp.where(live, home, 0.0).astype(jnp.int32)
    kind = pair[0:1] % SLOTS // K8
    behind = column - group
    size = NB // ROWS
    behind = jnp.where(behind > REACH, behind - size, jnp.where(behind < -REACH, behind + size, behind))
    behind = jnp.where(odd == 1, -behind, behind)
    piece = jnp.where(behind > 0, behind - 1, jnp.where(behind < 0, 1 - behind, 4))
    place_ref[...] = jnp.where(live, piece, 4) * ROWS + kind
    theirs = jnp.where(line == group * ROWS + kind, 1.0, 0.0).astype(BF16)
    far = jnp.dot(groups, theirs, preferred_element_type=F32)
    i = lax.broadcasted_iota(jnp.int32, (SLOTS, SLOTS), 0)
    j = lax.broadcasted_iota(jnp.int32, (SLOTS, SLOTS), 1)
    swap = jnp.where(i // K8 * K8 + 1 - i % K8 == j, 1.0, 0.0).astype(BF16)
    spread = jnp.where(slot == K8 * lax.axis_index("row") + pair // BLK, 1.0, 0.0).astype(BF16)
    facing = jnp.dot(swap, near.astype(BF16), preferred_element_type=F32)
    for ours, out_ref in ((near, same_ref), (facing, other_ref)):
        hit = jnp.where((far == ours) & (ours >= 0.0) & live, 1.0, 0.0).astype(BF16)
        mask = lax.dot_general(hit, spread, (((0,), (0,)), ((), ())), preferred_element_type=F32)
        for n in range(ROWS * SLOTS):
            out_ref[n] = jnp.broadcast_to(mask[n : n + 1], (16, WIDE)).astype(BF16)


def left_body(groups_ref, ground_ref, response_ref, out_ref, place_ref, same_ref, other_ref, turned):
    lookup(groups_ref, place_ref, same_ref, other_ref)
    src = lax.broadcasted_iota(jnp.int32, (256, 256), 0)
    dst = lax.broadcasted_iota(jnp.int32, (256, 256), 1)
    two, half, col = src // 128, src // BLK % 2, src % BLK
    want = half * 128 + two * BLK + (col % 2) * HALF + col // 2
    turn = jnp.where(dst == want, 1.0, 0.0).astype(BF16)
    for m, rows_ref in enumerate((response_ref, ground_ref)):

        def step(g, _, m=m, rows_ref=rows_ref):
            parts = by_slot(rows_ref, g, turned)
            pairs = [jnp.concatenate(parts[b : b + 2], axis=1) for b in range(0, SLOTS, 2)]
            both = jnp.dot(jnp.concatenate(pairs, axis=0), turn, preferred_element_type=F32).astype(BF16)
            for i in range(SLOTS // 2):
                piece = both[i * TILES : (i + 1) * TILES]
                out_ref[g, m * BLK : m * BLK + HALF, i * 128 : (i + 1) * 128] = piece[:, 0:128]
                out_ref[g, m * BLK + HALF : m * BLK + BLK, i * 128 : (i + 1) * 128] = piece[:, 128:256]
            return 0

        lax.fori_loop(0, ROWS, step, 0, unroll=True)


def fill_window(window, pieces):
    for o, piece in enumerate(pieces):
        for m in range(2):
            at = o * ROWS * BLK
            window[m, at : at + ROWS * BLK, :] = piece[m].reshape(ROWS * BLK, WIDE)


def rights(window, where_ref, same_ref, other_ref, g):
    stacks = ([], [])
    for a in range(SLOTS):
        i = g * SLOTS + a
        at = pl.multiple_of(where_ref[0, i] * BLK, BLK)
        same = jnp.concatenate([same_ref[i]] * 4, axis=0)
        other = jnp.concatenate([other_ref[i]] * 4, axis=0)
        for m in range(2):
            blocks = window[m, pl.ds(at, BLK), :]
            stacks[m].append(jnp.concatenate([blocks * same, blocks * other], axis=1))
    return [jnp.concatenate(stack, axis=0) for stack in stacks]


def settle(product):
    return product[:, 0:WIDE] + pltpu.roll(product[:, WIDE:], WIDE // 2, 1)


def first_body(where_ref, same_ref, other_ref, x0, x1, x2, x3, x4, left_ref, pair_ref, mixed_ref, window):
    fill_window(window, (x0, x1, x2, x3, x4))

    def step(g, _):
        ground, response = rights(window, where_ref, same_ref, other_ref, g)
        product = jnp.dot(left_ref[g], ground, preferred_element_type=F32)
        crossed = jnp.dot(left_ref[g, BLK:], response, preferred_element_type=F32)
        mixed = settle(product[0:BLK] + crossed)
        mixed_ref[g] = mixed
        pair_ref[0, g] = settle(product[BLK:]).astype(BF16)
        pair_ref[1, g] = mixed.astype(BF16)
        return 0

    lax.fori_loop(0, ROWS, step, 0, unroll=True)


def second_body(where_ref, same_ref, other_ref, x0, x1, x2, x3, x4, left_ref, mixed_ref, out_ref, window):
    fill_window(window, (x0, x1, x2, x3, x4))

    def step(g, _):
        square, mixed = rights(window, where_ref, same_ref, other_ref, g)
        cubic = jnp.dot(left_ref[g, 0:BLK], square, preferred_element_type=F32)
        cubic = settle(cubic + jnp.dot(left_ref[g, BLK:], mixed, preferred_element_type=F32))
        out_ref[g] = (3.0 * mixed_ref[g] - 2.0 * cubic).astype(BF16)
        return 0

    lax.fori_loop(0, ROWS, step, 0, unroll=True)


def join_body(in_ref, out_ref, turned):
    for r in range(ROWS):
        first, second = in_ref[r, 0:HALF].astype(F32), in_ref[r, HALF:BLK].astype(F32)
        for i, lines in enumerate(cross(first, second)):
            turned[pl.ds((K8 * r + i) * TILES, TILES), :] = lines
    for t in range(TILES):
        out_ref[0, :, t * 128 : (t + 1) * 128] = turned[pl.ds(t, SLOTS, stride=TILES), :].astype(BF16)


def from_afar(block, distance):
    columns, rows = lax.axis_size("col"), lax.axis_size("row")
    route = []
    for c in range(columns):
        for r in range(rows):
            to = (c + (distance if r % 2 == 0 else -distance)) % columns
            route.append((c * rows + r, to * rows + r))
    return lax.ppermute(block, ("col", "row"), route)


def surround(block):
    return [from_afar(block, distance) for distance in (1, 2, -1, -2)] + [block]


def local(ground, response, pattern):
    rows = jax.ShapeDtypeStruct((2, ROWS, BLK, WIDE), BF16)
    mask = jax.ShapeDtypeStruct((ROWS * SLOTS, 16, WIDE), BF16)
    smem = pl.BlockSpec(memory_space=pltpu.SMEM)
    turned = pltpu.VMEM((SLOTS * TILES, 128), F32)
    window = pltpu.VMEM((2, 5 * ROWS * BLK, WIDE), BF16)
    cut = call(
        slice_body,
        "slice",
        rows,
        [
            pltpu.VMEM((2, ROWS, SLOTS, BLK * BLK), BF16),
            pltpu.VMEM((2, 2, ROWS * HALF, 128), F32),
            pltpu.SemaphoreType.DMA((2,)),
        ],
        [pl.BlockSpec(memory_space=pltpu.HBM)] * 2,
        2 * 2 * 16 * 128 * 4096,
        5 << 20,
        SLICE_BYTES,
    )(ground, response)
    cut, ground, response, pattern = lax.optimization_barrier((cut, ground, response, pattern))
    pieces = surround(cut)
    groups = jnp.where(pattern < 0, -1, pattern // ROWS).T
    left, place, same, other = call(
        left_body,
        "left",
        (jax.ShapeDtypeStruct((ROWS, 2 * BLK, SLOTS * BLK), BF16), jax.ShapeDtypeStruct((1, WIDE), jnp.int32), mask, mask),
        [turned],
        in_vmem(3),
        2 * 4096 * 256 * 256,
        5 << 20,
    )(groups, ground, response)
    flops = 2 * ROWS * BLK * 1024 * 128
    pair, mixed = call(
        first_body,
        "first",
        (rows, jax.ShapeDtypeStruct((ROWS, BLK, WIDE), F32)),
        [window],
        [smem] + in_vmem(8),
        3 * flops,
        5 << 20,
    )(place, same, other, *pieces, left)
    pieces = surround(pair)
    part = call(
        second_body,
        "second",
        jax.ShapeDtypeStruct((ROWS, BLK, WIDE), BF16),
        [window],
        [smem] + in_vmem(9),
        2 * flops,
        5 << 20,
    )(place, same, other, *pieces, left, mixed)
    part = lax.all_to_all(part, "row", 0, 0, tiled=True)
    return call(
        join_body,
        "join",
        jax.ShapeDtypeStruct((1, SLOTS, BLK * BLK), BF16),
        [turned],
        in_vmem(1),
        0,
        1 << 18,
    )(part)


def solution(mesh):
    in_specs = (P("col", None, None), P("col", None, None), P())
    out_specs = P(("col", "row"), None, None)
    return jax.shard_map(local, mesh=mesh, in_specs=in_specs, out_specs=out_specs, check_vma=False)
```

```python
import jax
import jax.numpy as jnp
from jax import lax
from jax.experimental import pallas as pl
from jax.experimental.pallas import tpu as pltpu
from jax.sharding import PartitionSpec as P

BLK = 64
K8 = 2
REACH = 2
NB = 512
SLOTS = 16
ROWS = 8
WIDE = K8 * BLK
TILES = BLK * BLK // 128
HALF = TILES
F32, BF16 = jnp.float32, jnp.bfloat16
VMEM_BYTES = 16 * 1024 * 1024


SLICE_BYTES = int(8 * 1024 * 1024)


def call(body, name, out_shape, scratch, in_specs, flops, moved, vmem=VMEM_BYTES):
    del name
    return pl.pallas_call(
        body,
        out_shape=out_shape,
        in_specs=in_specs,
        out_specs=jax.tree.map(lambda _: pl.BlockSpec(memory_space=pltpu.VMEM), out_shape),
        scratch_shapes=scratch,
        compiler_params=pltpu.CompilerParams(vmem_limit_bytes=vmem),
        cost_estimate=pl.CostEstimate(flops=flops, bytes_accessed=moved, transcendentals=0),
    )


def in_vmem(count):
    return [pl.BlockSpec(memory_space=pltpu.VMEM)] * count


def by_slot(rows_ref, g, turned):
    flat = rows_ref[g]
    for t in range(TILES):
        turned[pl.ds(t * SLOTS, SLOTS), :] = flat[:, t * 128 : (t + 1) * 128].astype(F32)
    return [turned[pl.ds(b, TILES, stride=SLOTS), :].astype(BF16) for b in range(SLOTS)]


def cross(a, b):
    low = lax.broadcasted_iota(jnp.int32, a.shape, 1) < BLK
    return jnp.where(low, a, pltpu.roll(b, BLK, 1)), jnp.where(low, pltpu.roll(a, BLK, 1), b)


def fetch(sources, held, arrived):
    copies = [pltpu.make_async_copy(source, held.at[m], arrived.at[m]) for m, source in enumerate(sources)]
    for copy in copies:
        copy.start()
    return copies


def slice_body(ground_hbm, response_hbm, out_ref, held, placed, arrived):
    copies = fetch((ground_hbm, response_hbm), held, arrived)
    line = lax.broadcasted_iota(jnp.int32, (K8 * ROWS, ROWS * SLOTS), 0)
    slot = lax.broadcasted_iota(jnp.int32, (K8 * ROWS, ROWS * SLOTS), 1)
    want = line % ROWS * SLOTS + K8 * lax.axis_index("row") + line // ROWS
    pick = jnp.where(slot == want, 1.0, 0.0).astype(BF16)
    for m in range(2):
        copies[m].wait()
        flat = held[m].reshape(ROWS * SLOTS, BLK * BLK)
        mine = jnp.dot(pick, flat, preferred_element_type=F32)
        for t in range(TILES):
            part = mine[:, t * 128 : (t + 1) * 128]
            for half, lines in enumerate(cross(part[0:ROWS], part[ROWS:])):
                placed[m, half, pl.ds(t, ROWS, stride=HALF), :] = lines
        for half in range(2):
            lines = placed[m, half].astype(BF16).reshape(ROWS, HALF, 128)
            out_ref[m, :, half * HALF : (half + 1) * HALF, :] = lines


def lookup(groups_ref, place_ref, same_ref, other_ref):
    column, odd = lax.axis_index("col"), lax.axis_index("row") % 2
    groups = groups_ref[...].astype(F32).astype(BF16)
    line = lax.broadcasted_iota(jnp.int32, (NB, WIDE), 0)
    lane = lax.broadcasted_iota(jnp.int32, (NB, WIDE), 1)
    mine = jnp.where(line == column * ROWS + lane // SLOTS, 1.0, 0.0).astype(BF16)
    near = jnp.dot(groups, mine, preferred_element_type=F32)
    slot = lax.broadcasted_iota(jnp.int32, (SLOTS, WIDE), 0)
    pair = lax.broadcasted_iota(jnp.int32, (SLOTS, WIDE), 1)
    home = jnp.sum(jnp.where(slot == pair % SLOTS, near, 0.0), axis=0, keepdims=True)
    live = home >= 0.0
    group = jnp.where(live, home, 0.0).astype(jnp.int32)
    kind = pair[0:1] % SLOTS // K8
    behind = column - group
    size = NB // ROWS
    behind = jnp.where(behind > REACH, behind - size, jnp.where(behind < -REACH, behind + size, behind))
    behind = jnp.where(odd == 1, -behind, behind)
    piece = jnp.where(behind > 0, behind - 1, jnp.where(behind < 0, 1 - behind, 4))
    place_ref[...] = jnp.where(live, piece, 4) * ROWS + kind
    theirs = jnp.where(line == group * ROWS + kind, 1.0, 0.0).astype(BF16)
    far = jnp.dot(groups, theirs, preferred_element_type=F32)
    i = lax.broadcasted_iota(jnp.int32, (SLOTS, SLOTS), 0)
    j = lax.broadcasted_iota(jnp.int32, (SLOTS, SLOTS), 1)
    swap = jnp.where(i // K8 * K8 + 1 - i % K8 == j, 1.0, 0.0).astype(BF16)
    spread = jnp.where(slot == K8 * lax.axis_index("row") + pair // BLK, 1.0, 0.0).astype(BF16)
    facing = jnp.dot(swap, near.astype(BF16), preferred_element_type=F32)
    for ours, out_ref in ((near, same_ref), (facing, other_ref)):
        hit = jnp.where((far == ours) & (ours >= 0.0) & live, 1.0, 0.0).astype(BF16)
        mask = lax.dot_general(hit, spread, (((0,), (0,)), ((), ())), preferred_element_type=F32)
        for n in range(ROWS * SLOTS):
            out_ref[n] = jnp.broadcast_to(mask[n : n + 1], (16, WIDE)).astype(BF16)


def left_body(groups_ref, ground_hbm, response_hbm, out_ref, place_ref, same_ref, other_ref, turned, held, arrived):
    copies = fetch((response_hbm, ground_hbm), held, arrived)
    lookup(groups_ref, place_ref, same_ref, other_ref)
    src = lax.broadcasted_iota(jnp.int32, (256, 256), 0)
    dst = lax.broadcasted_iota(jnp.int32, (256, 256), 1)
    two, half, col = src // 128, src // BLK % 2, src % BLK
    want = half * 128 + two * BLK + (col % 2) * HALF + col // 2
    turn = jnp.where(dst == want, 1.0, 0.0).astype(BF16)
    for m in range(2):
        copies[m].wait()

        def step(g, _, m=m):
            parts = by_slot(held.at[m], g, turned)
            pairs = [jnp.concatenate(parts[b : b + 2], axis=1) for b in range(0, SLOTS, 2)]
            both = jnp.dot(jnp.concatenate(pairs, axis=0), turn, preferred_element_type=F32).astype(BF16)
            for i in range(SLOTS // 2):
                piece = both[i * TILES : (i + 1) * TILES]
                out_ref[g, m * BLK : m * BLK + HALF, i * 128 : (i + 1) * 128] = piece[:, 0:128]
                out_ref[g, m * BLK + HALF : m * BLK + BLK, i * 128 : (i + 1) * 128] = piece[:, 128:256]
            return 0

        lax.fori_loop(0, ROWS, step, 0, unroll=True)


def fill_window(window, pieces):
    for o, piece in enumerate(pieces):
        for m in range(2):
            at = o * ROWS * BLK
            window[m, at : at + ROWS * BLK, :] = piece[m].reshape(ROWS * BLK, WIDE)


def rights(window, where_ref, same_ref, other_ref, g):
    stacks = ([], [])
    for a in range(SLOTS):
        i = g * SLOTS + a
        at = pl.multiple_of(where_ref[0, i] * BLK, BLK)
        same = jnp.concatenate([same_ref[i]] * 4, axis=0)
        other = jnp.concatenate([other_ref[i]] * 4, axis=0)
        for m in range(2):
            blocks = window[m, pl.ds(at, BLK), :]
            stacks[m].append(jnp.concatenate([blocks * same, blocks * other], axis=1))
    return [jnp.concatenate(stack, axis=0) for stack in stacks]


def settle(product):
    return product[:, 0:WIDE] + pltpu.roll(product[:, WIDE:], WIDE // 2, 1)


def first_body(where_ref, same_ref, other_ref, x0, x1, x2, x3, x4, left_ref, pair_ref, mixed_ref, window):
    fill_window(window, (x0, x1, x2, x3, x4))

    def step(g, _):
        ground, response = rights(window, where_ref, same_ref, other_ref, g)
        product = jnp.dot(left_ref[g], ground, preferred_element_type=F32)
        crossed = jnp.dot(left_ref[g, BLK:], response, preferred_element_type=F32)
        mixed = settle(product[0:BLK] + crossed)
        mixed_ref[g] = mixed
        pair_ref[0, g] = settle(product[BLK:]).astype(BF16)
        pair_ref[1, g] = mixed.astype(BF16)
        return 0

    lax.fori_loop(0, ROWS, step, 0, unroll=True)


def second_body(where_ref, same_ref, other_ref, x0, x1, x2, x3, x4, left_ref, mixed_ref, out_ref, window):
    fill_window(window, (x0, x1, x2, x3, x4))

    def step(g, _):
        square, mixed = rights(window, where_ref, same_ref, other_ref, g)
        cubic = jnp.dot(left_ref[g, 0:BLK], square, preferred_element_type=F32)
        cubic = settle(cubic + jnp.dot(left_ref[g, BLK:], mixed, preferred_element_type=F32))
        out_ref[g] = (3.0 * mixed_ref[g] - 2.0 * cubic).astype(BF16)
        return 0

    lax.fori_loop(0, ROWS, step, 0, unroll=True)


def join_body(in_ref, out_ref, turned):
    for r in range(ROWS):
        first, second = in_ref[r, 0:HALF].astype(F32), in_ref[r, HALF:BLK].astype(F32)
        for i, lines in enumerate(cross(first, second)):
            turned[pl.ds((K8 * r + i) * TILES, TILES), :] = lines
    for t in range(TILES):
        out_ref[0, :, t * 128 : (t + 1) * 128] = turned[pl.ds(t, SLOTS, stride=TILES), :].astype(BF16)


def from_afar(block, distance):
    columns, rows = lax.axis_size("col"), lax.axis_size("row")
    route = []
    for c in range(columns):
        for r in range(rows):
            to = (c + (distance if r % 2 == 0 else -distance)) % columns
            route.append((c * rows + r, to * rows + r))
    return lax.ppermute(block, ("col", "row"), route)


def surround(block):
    return [from_afar(block, distance) for distance in (1, 2, -1, -2)] + [block]


def local(ground, response, pattern):
    rows = jax.ShapeDtypeStruct((2, ROWS, BLK, WIDE), BF16)
    mask = jax.ShapeDtypeStruct((ROWS * SLOTS, 16, WIDE), BF16)
    smem = pl.BlockSpec(memory_space=pltpu.SMEM)
    turned = pltpu.VMEM((SLOTS * TILES, 128), F32)
    held = pltpu.VMEM((2, ROWS, SLOTS, BLK * BLK), BF16)
    window = pltpu.VMEM((2, 5 * ROWS * BLK, WIDE), BF16)
    ground, response = (pltpu.with_memory_space_constraint(x, pltpu.HBM) for x in (ground, response))
    cut = call(
        slice_body,
        "slice",
        rows,
        [
            held,
            pltpu.VMEM((2, 2, ROWS * HALF, 128), F32),
            pltpu.SemaphoreType.DMA((2,)),
        ],
        [pl.BlockSpec(memory_space=pltpu.HBM)] * 2,
        2 * 2 * 16 * 128 * 4096,
        5 << 20,
        SLICE_BYTES,
    )(ground, response)
    cut, ground, response, pattern = lax.optimization_barrier((cut, ground, response, pattern))
    pieces = surround(cut)
    groups = jnp.where(pattern < 0, -1, pattern // ROWS).T
    left, place, same, other = call(
        left_body,
        "left",
        (jax.ShapeDtypeStruct((ROWS, 2 * BLK, SLOTS * BLK), BF16), jax.ShapeDtypeStruct((1, WIDE), jnp.int32), mask, mask),
        [turned, held, pltpu.SemaphoreType.DMA((2,))],
        in_vmem(1) + [pl.BlockSpec(memory_space=pltpu.HBM)] * 2,
        2 * 4096 * 256 * 256,
        5 << 20,
    )(groups, ground, response)
    flops = 2 * ROWS * BLK * 1024 * 128
    pair, mixed = call(
        first_body,
        "first",
        (rows, jax.ShapeDtypeStruct((ROWS, BLK, WIDE), F32)),
        [window],
        [smem] + in_vmem(8),
        3 * flops,
        5 << 20,
    )(place, same, other, *pieces, left)
    pieces = surround(pair)
    part = call(
        second_body,
        "second",
        jax.ShapeDtypeStruct((ROWS, BLK, WIDE), BF16),
        [window],
        [smem] + in_vmem(9),
        2 * flops,
        5 << 20,
    )(place, same, other, *pieces, left, mixed)
    part = lax.all_to_all(part, "row", 0, 0, tiled=True)
    return call(
        join_body,
        "join",
        jax.ShapeDtypeStruct((1, SLOTS, BLK * BLK), BF16),
        [turned],
        in_vmem(1),
        0,
        1 << 18,
    )(part)


def solution(mesh):
    in_specs = (P("col", None, None), P("col", None, None), P())
    out_specs = P(("col", "row"), None, None)
    return jax.shard_map(local, mesh=mesh, in_specs=in_specs, out_specs=out_specs, check_vma=False)
```

```python
import jax
import jax.numpy as jnp
from jax import lax
from jax.experimental import pallas as pl
from jax.experimental.pallas import tpu as pltpu
from jax.sharding import PartitionSpec as P

BLK = 64
K8 = 2
REACH = 2
NB = 512
SLOTS = 16
ROWS = 8
WIDE = K8 * BLK
TILES = BLK * BLK // 128
HALF = TILES
F32, BF16 = jnp.float32, jnp.bfloat16
VMEM_BYTES = 16 * 1024 * 1024


SLICE_BYTES = 8 * 1024 * 1024


def call(body, name, out_shape, scratch, in_specs, flops, moved, vmem=VMEM_BYTES):
    del name
    return pl.pallas_call(
        body,
        out_shape=out_shape,
        in_specs=in_specs,
        out_specs=jax.tree.map(lambda _: pl.BlockSpec(memory_space=pltpu.VMEM), out_shape),
        scratch_shapes=scratch,
        compiler_params=pltpu.CompilerParams(vmem_limit_bytes=vmem),
        cost_estimate=pl.CostEstimate(flops=flops, bytes_accessed=moved, transcendentals=0),
    )


def in_vmem(count):
    return [pl.BlockSpec(memory_space=pltpu.VMEM)] * count


def by_slot(rows_ref, g, turned):
    flat = rows_ref[g]
    for t in range(TILES):
        turned[pl.ds(t * SLOTS, SLOTS), :] = flat[:, t * 128 : (t + 1) * 128].astype(F32)
    return [turned[pl.ds(b, TILES, stride=SLOTS), :].astype(BF16) for b in range(SLOTS)]


def cross(a, b):
    low = lax.broadcasted_iota(jnp.int32, a.shape, 1) < BLK
    return jnp.where(low, a, pltpu.roll(b, BLK, 1)), jnp.where(low, pltpu.roll(a, BLK, 1), b)


def fetch(sources, held, arrived):
    copies = [pltpu.make_async_copy(source, held.at[m], arrived.at[m]) for m, source in enumerate(sources)]
    for copy in copies:
        copy.start()
    return copies


def slice_body(ground_hbm, response_hbm, out_ref, held, placed, arrived):
    copies = fetch((ground_hbm, response_hbm), held, arrived)
    line = lax.broadcasted_iota(jnp.int32, (K8 * ROWS, ROWS * SLOTS), 0)
    slot = lax.broadcasted_iota(jnp.int32, (K8 * ROWS, ROWS * SLOTS), 1)
    want = line % ROWS * SLOTS + K8 * lax.axis_index("row") + line // ROWS
    pick = jnp.where(slot == want, 1.0, 0.0).astype(BF16)
    for m in range(2):
        copies[m].wait()
        flat = held[m].reshape(ROWS * SLOTS, BLK * BLK)
        mine = jnp.dot(pick, flat, preferred_element_type=F32)
        for t in range(TILES):
            part = mine[:, t * 128 : (t + 1) * 128]
            for half, lines in enumerate(cross(part[0:ROWS], part[ROWS:])):
                placed[m, half, pl.ds(t, ROWS, stride=HALF), :] = lines
        for half in range(2):
            lines = placed[m, half].astype(BF16).reshape(ROWS, HALF, 128)
            out_ref[m, :, half * HALF : (half + 1) * HALF, :] = lines


def lookup(groups_ref, place_ref, same_ref, other_ref):
    column, odd = lax.axis_index("col"), lax.axis_index("row") % 2
    groups = groups_ref[...].astype(F32).astype(BF16)
    line = lax.broadcasted_iota(jnp.int32, (NB, WIDE), 0)
    lane = lax.broadcasted_iota(jnp.int32, (NB, WIDE), 1)
    mine = jnp.where(line == column * ROWS + lane // SLOTS, 1.0, 0.0).astype(BF16)
    near = jnp.dot(groups, mine, preferred_element_type=F32)
    slot = lax.broadcasted_iota(jnp.int32, (SLOTS, WIDE), 0)
    pair = lax.broadcasted_iota(jnp.int32, (SLOTS, WIDE), 1)
    home = jnp.sum(jnp.where(slot == pair % SLOTS, near, 0.0), axis=0, keepdims=True)
    live = home >= 0.0
    group = jnp.where(live, home, 0.0).astype(jnp.int32)
    kind = pair[0:1] % SLOTS // K8
    behind = column - group
    size = NB // ROWS
    behind = jnp.where(behind > REACH, behind - size, jnp.where(behind < -REACH, behind + size, behind))
    ahead = jnp.where(behind < 0, 1, 0)
    twice = jnp.where(behind > 1, 1, jnp.where(behind < -1, 1, 0))
    low = twice * (1 - column % 4 // 2) + (1 - twice) * (1 - column % 2)
    plain = 1 - jnp.abs(ahead - low)
    piece = jnp.where(behind == 0, 4, 2 * twice + plain + odd * (1 - 2 * plain))
    place_ref[...] = jnp.where(live, piece, 4) * ROWS + kind
    theirs = jnp.where(line == group * ROWS + kind, 1.0, 0.0).astype(BF16)
    far = jnp.dot(groups, theirs, preferred_element_type=F32)
    i = lax.broadcasted_iota(jnp.int32, (SLOTS, SLOTS), 0)
    j = lax.broadcasted_iota(jnp.int32, (SLOTS, SLOTS), 1)
    swap = jnp.where(i // K8 * K8 + 1 - i % K8 == j, 1.0, 0.0).astype(BF16)
    spread = jnp.where(slot == K8 * lax.axis_index("row") + pair // BLK, 1.0, 0.0).astype(BF16)
    facing = jnp.dot(swap, near.astype(BF16), preferred_element_type=F32)
    for ours, out_ref in ((near, same_ref), (facing, other_ref)):
        hit = jnp.where((far == ours) & (ours >= 0.0) & live, 1.0, 0.0).astype(BF16)
        mask = lax.dot_general(hit, spread, (((0,), (0,)), ((), ())), preferred_element_type=F32)
        for n in range(ROWS * SLOTS):
            out_ref[n] = jnp.broadcast_to(mask[n : n + 1], (16, WIDE)).astype(BF16)


def left_body(groups_ref, ground_hbm, response_hbm, out_ref, place_ref, same_ref, other_ref, turned, held, arrived):
    copies = fetch((response_hbm, ground_hbm), held, arrived)
    lookup(groups_ref, place_ref, same_ref, other_ref)
    src = lax.broadcasted_iota(jnp.int32, (256, 256), 0)
    dst = lax.broadcasted_iota(jnp.int32, (256, 256), 1)
    two, half, col = src // 128, src // BLK % 2, src % BLK
    want = half * 128 + two * BLK + (col % 2) * HALF + col // 2
    turn = jnp.where(dst == want, 1.0, 0.0).astype(BF16)
    for m in range(2):
        copies[m].wait()

        def step(g, _, m=m):
            parts = by_slot(held.at[m], g, turned)
            pairs = [jnp.concatenate(parts[b : b + 2], axis=1) for b in range(0, SLOTS, 2)]
            both = jnp.dot(jnp.concatenate(pairs, axis=0), turn, preferred_element_type=F32).astype(BF16)
            for i in range(SLOTS // 2):
                piece = both[i * TILES : (i + 1) * TILES]
                out_ref[g, m * BLK : m * BLK + HALF, i * 128 : (i + 1) * 128] = piece[:, 0:128]
                out_ref[g, m * BLK + HALF : m * BLK + BLK, i * 128 : (i + 1) * 128] = piece[:, 128:256]
            return 0

        lax.fori_loop(0, ROWS, step, 0, unroll=True)


def fill_window(window, pieces):
    for o, piece in enumerate(pieces):
        for m in range(2):
            at = o * ROWS * BLK
            window[m, at : at + ROWS * BLK, :] = piece[m].reshape(ROWS * BLK, WIDE)


def rights(window, where_ref, same_ref, other_ref, g):
    stacks = ([], [])
    for a in range(SLOTS):
        i = g * SLOTS + a
        at = pl.multiple_of(where_ref[0, i] * BLK, BLK)
        same = jnp.concatenate([same_ref[i]] * 4, axis=0)
        other = jnp.concatenate([other_ref[i]] * 4, axis=0)
        for m in range(2):
            blocks = window[m, pl.ds(at, BLK), :]
            stacks[m].append(jnp.concatenate([blocks * same, blocks * other], axis=1))
    return [jnp.concatenate(stack, axis=0) for stack in stacks]


def settle(product):
    return product[:, 0:WIDE] + pltpu.roll(product[:, WIDE:], WIDE // 2, 1)


def first_body(where_ref, same_ref, other_ref, x0, x1, x2, x3, x4, left_ref, pair_ref, mixed_ref, window):
    fill_window(window, (x0, x1, x2, x3, x4))

    def step(g, _):
        ground, response = rights(window, where_ref, same_ref, other_ref, g)
        product = jnp.dot(left_ref[g], ground, preferred_element_type=F32)
        crossed = jnp.dot(left_ref[g, BLK:], response, preferred_element_type=F32)
        mixed = settle(product[0:BLK] + crossed)
        mixed_ref[g] = mixed
        pair_ref[0, g] = settle(product[BLK:]).astype(BF16)
        pair_ref[1, g] = mixed.astype(BF16)
        return 0

    lax.fori_loop(0, ROWS, step, 0, unroll=True)


def second_body(where_ref, same_ref, other_ref, x0, x1, x2, x3, x4, left_ref, mixed_ref, out_ref, window):
    fill_window(window, (x0, x1, x2, x3, x4))

    def step(g, _):
        square, mixed = rights(window, where_ref, same_ref, other_ref, g)
        cubic = jnp.dot(left_ref[g, 0:BLK], square, preferred_element_type=F32)
        cubic = settle(cubic + jnp.dot(left_ref[g, BLK:], mixed, preferred_element_type=F32))
        out_ref[g] = (3.0 * mixed_ref[g] - 2.0 * cubic).astype(BF16)
        return 0

    lax.fori_loop(0, ROWS, step, 0, unroll=True)


def join_body(in_ref, out_ref, turned):
    for r in range(ROWS):
        first, second = in_ref[r, 0:HALF].astype(F32), in_ref[r, HALF:BLK].astype(F32)
        for i, lines in enumerate(cross(first, second)):
            turned[pl.ds((K8 * r + i) * TILES, TILES), :] = lines
    for t in range(TILES):
        out_ref[0, :, t * 128 : (t + 1) * 128] = turned[pl.ds(t, SLOTS, stride=TILES), :].astype(BF16)


def partner(column, distance, shifted):
    size = NB // ROWS
    back = distance if shifted else 0
    return (((column - back) % size ^ distance) + back) % size


def trade(block, distance, shifted):
    columns, rows = lax.axis_size("col"), lax.axis_size("row")
    route = []
    for c in range(columns):
        for r in range(rows):
            route.append((c * rows + r, partner(c, distance, shifted != (r % 2 == 1)) * rows + r))
    return lax.ppermute(block, ("col", "row"), route)


def surround(block):
    return [trade(block, distance, shifted) for distance in (1, 2) for shifted in (True, False)] + [block]


def local(ground, response, pattern):
    rows = jax.ShapeDtypeStruct((2, ROWS, BLK, WIDE), BF16)
    mask = jax.ShapeDtypeStruct((ROWS * SLOTS, 16, WIDE), BF16)
    smem = pl.BlockSpec(memory_space=pltpu.SMEM)
    turned = pltpu.VMEM((SLOTS * TILES, 128), F32)
    held = pltpu.VMEM((2, ROWS, SLOTS, BLK * BLK), BF16)
    window = pltpu.VMEM((2, 5 * ROWS * BLK, WIDE), BF16)
    ground, response = (pltpu.with_memory_space_constraint(x, pltpu.HBM) for x in (ground, response))
    cut = call(
        slice_body,
        "slice",
        rows,
        [
            held,
            pltpu.VMEM((2, 2, ROWS * HALF, 128), F32),
            pltpu.SemaphoreType.DMA((2,)),
        ],
        [pl.BlockSpec(memory_space=pltpu.HBM)] * 2,
        2 * 2 * 16 * 128 * 4096,
        5 << 20,
        SLICE_BYTES,
    )(ground, response)
    cut, ground, response, pattern = lax.optimization_barrier((cut, ground, response, pattern))
    pieces = surround(cut)
    groups = jnp.where(pattern < 0, -1, pattern // ROWS).T
    left, place, same, other = call(
        left_body,
        "left",
        (jax.ShapeDtypeStruct((ROWS, 2 * BLK, SLOTS * BLK), BF16), jax.ShapeDtypeStruct((1, WIDE), jnp.int32), mask, mask),
        [turned, held, pltpu.SemaphoreType.DMA((2,))],
        in_vmem(1) + [pl.BlockSpec(memory_space=pltpu.HBM)] * 2,
        2 * 4096 * 256 * 256,
        5 << 20,
    )(groups, ground, response)
    flops = 2 * ROWS * BLK * 1024 * 128
    pair, mixed = call(
        first_body,
        "first",
        (rows, jax.ShapeDtypeStruct((ROWS, BLK, WIDE), F32)),
        [window],
        [smem] + in_vmem(8),
        3 * flops,
        5 << 20,
    )(place, same, other, *pieces, left)
    pieces = surround(pair)
    part = call(
        second_body,
        "second",
        jax.ShapeDtypeStruct((ROWS, BLK, WIDE), BF16),
        [window],
        [smem] + in_vmem(9),
        2 * flops,
        5 << 20,
    )(place, same, other, *pieces, left, mixed)
    part = lax.all_to_all(part, "row", 0, 0, tiled=True)
    return call(
        join_body,
        "join",
        jax.ShapeDtypeStruct((1, SLOTS, BLK * BLK), BF16),
        [turned],
        in_vmem(1),
        0,
        1 << 18,
    )(part)


def solution(mesh):
    in_specs = (P("col", None, None), P("col", None, None), P())
    out_specs = P(("col", "row"), None, None)
    return jax.shard_map(local, mesh=mesh, in_specs=in_specs, out_specs=out_specs, check_vma=False)
```

```python
import jax
import jax.numpy as jnp
from jax import lax
from jax.experimental import pallas as pl
from jax.experimental.pallas import tpu as pltpu
from jax.sharding import PartitionSpec as P

BLK = 64
K8 = 2
REACH = 2
NB = 512
SLOTS = 16
ROWS = 8
WIDE = K8 * BLK
TILES = BLK * BLK // 128
HALF = TILES
F32, BF16 = jnp.float32, jnp.bfloat16
VMEM_BYTES = 16 * 1024 * 1024


SLICE_BYTES = 8 * 1024 * 1024


def call(body, name, out_shape, scratch, in_specs, flops, moved, vmem=VMEM_BYTES):
    del name
    return pl.pallas_call(
        body,
        out_shape=out_shape,
        in_specs=in_specs,
        out_specs=jax.tree.map(lambda _: pl.BlockSpec(memory_space=pltpu.VMEM), out_shape),
        scratch_shapes=scratch,
        compiler_params=pltpu.CompilerParams(vmem_limit_bytes=vmem),
        cost_estimate=pl.CostEstimate(flops=flops, bytes_accessed=moved, transcendentals=0),
    )


def in_vmem(count):
    return [pl.BlockSpec(memory_space=pltpu.VMEM)] * count


def by_slot(rows_ref, g, turned):
    flat = rows_ref[g]
    for t in range(TILES):
        turned[pl.ds(t * SLOTS, SLOTS), :] = flat[:, t * 128 : (t + 1) * 128].astype(F32)
    return [turned[pl.ds(b, TILES, stride=SLOTS), :].astype(BF16) for b in range(SLOTS)]


def cross(a, b):
    low = lax.broadcasted_iota(jnp.int32, a.shape, 1) < BLK
    return jnp.where(low, a, pltpu.roll(b, BLK, 1)), jnp.where(low, pltpu.roll(a, BLK, 1), b)


def fetch(sources, held, arrived):
    copies = [pltpu.make_async_copy(source, held.at[m], arrived.at[m]) for m, source in enumerate(sources)]
    for copy in copies:
        copy.start()
    return copies


def slice_body(ground_hbm, response_hbm, out_ref, held, placed, arrived):
    copies = fetch((ground_hbm, response_hbm), held, arrived)
    line = lax.broadcasted_iota(jnp.int32, (K8 * ROWS, ROWS * SLOTS), 0)
    slot = lax.broadcasted_iota(jnp.int32, (K8 * ROWS, ROWS * SLOTS), 1)
    want = line % ROWS * SLOTS + K8 * lax.axis_index("row") + line // ROWS
    pick = jnp.where(slot == want, 1.0, 0.0).astype(BF16)
    for m in range(2):
        copies[m].wait()
        flat = held[m].reshape(ROWS * SLOTS, BLK * BLK)
        mine = jnp.dot(pick, flat, preferred_element_type=F32)
        for t in range(TILES):
            part = mine[:, t * 128 : (t + 1) * 128]
            for half, lines in enumerate(cross(part[0:ROWS], part[ROWS:])):
                placed[m, half, pl.ds(t, ROWS, stride=HALF), :] = lines
        for half in range(2):
            lines = placed[m, half].astype(BF16).reshape(ROWS, HALF, 128)
            out_ref[m, :, half * HALF : (half + 1) * HALF, :] = lines


def lookup(groups_ref, place_ref, same_ref, other_ref):
    column, odd = lax.axis_index("col"), lax.axis_index("row") % 2
    groups = groups_ref[...].astype(F32).astype(BF16)
    line = lax.broadcasted_iota(jnp.int32, (NB, WIDE), 0)
    lane = lax.broadcasted_iota(jnp.int32, (NB, WIDE), 1)
    mine = jnp.where(line == column * ROWS + lane // SLOTS, 1.0, 0.0).astype(BF16)
    near = jnp.dot(groups, mine, preferred_element_type=F32)
    slot = lax.broadcasted_iota(jnp.int32, (SLOTS, WIDE), 0)
    pair = lax.broadcasted_iota(jnp.int32, (SLOTS, WIDE), 1)
    home = jnp.sum(jnp.where(slot == pair % SLOTS, near, 0.0), axis=0, keepdims=True)
    live = home >= 0.0
    group = jnp.where(live, home, 0.0).astype(jnp.int32)
    kind = pair[0:1] % SLOTS // K8
    behind = column - group
    size = NB // ROWS
    behind = jnp.where(behind > REACH, behind - size, jnp.where(behind < -REACH, behind + size, behind))
    ahead = jnp.where(behind < 0, 1, 0)
    twice = jnp.where(behind > 1, 1, jnp.where(behind < -1, 1, 0))
    low = twice * (1 - column % 4 // 2) + (1 - twice) * (1 - column % 2)
    plain = 1 - jnp.abs(ahead - low)
    plain = plain + odd * (1 - 2 * plain)
    piece = jnp.where(behind == 0, 4, jnp.where(twice == 1, 2 + plain, 1 - plain))
    place_ref[...] = jnp.where(live, piece, 4) * ROWS + kind
    theirs = jnp.where(line == group * ROWS + kind, 1.0, 0.0).astype(BF16)
    far = jnp.dot(groups, theirs, preferred_element_type=F32)
    i = lax.broadcasted_iota(jnp.int32, (SLOTS, SLOTS), 0)
    j = lax.broadcasted_iota(jnp.int32, (SLOTS, SLOTS), 1)
    swap = jnp.where(i // K8 * K8 + 1 - i % K8 == j, 1.0, 0.0).astype(BF16)
    spread = jnp.where(slot == K8 * lax.axis_index("row") + pair // BLK, 1.0, 0.0).astype(BF16)
    facing = jnp.dot(swap, near.astype(BF16), preferred_element_type=F32)
    for ours, out_ref in ((near, same_ref), (facing, other_ref)):
        hit = jnp.where((far == ours) & (ours >= 0.0) & live, 1.0, 0.0).astype(BF16)
        mask = lax.dot_general(hit, spread, (((0,), (0,)), ((), ())), preferred_element_type=F32)
        for n in range(ROWS * SLOTS):
            out_ref[n] = jnp.broadcast_to(mask[n : n + 1], (16, WIDE)).astype(BF16)


def left_body(groups_ref, ground_hbm, response_hbm, out_ref, place_ref, same_ref, other_ref, turned, held, arrived):
    copies = fetch((response_hbm, ground_hbm), held, arrived)
    lookup(groups_ref, place_ref, same_ref, other_ref)
    src = lax.broadcasted_iota(jnp.int32, (256, 256), 0)
    dst = lax.broadcasted_iota(jnp.int32, (256, 256), 1)
    two, half, col = src // 128, src // BLK % 2, src % BLK
    want = half * 128 + two * BLK + (col % 2) * HALF + col // 2
    turn = jnp.where(dst == want, 1.0, 0.0).astype(BF16)
    for m in range(2):
        copies[m].wait()

        def step(g, _, m=m):
            parts = by_slot(held.at[m], g, turned)
            pairs = [jnp.concatenate(parts[b : b + 2], axis=1) for b in range(0, SLOTS, 2)]
            both = jnp.dot(jnp.concatenate(pairs, axis=0), turn, preferred_element_type=F32).astype(BF16)
            for i in range(SLOTS // 2):
                piece = both[i * TILES : (i + 1) * TILES]
                out_ref[g, m * BLK : m * BLK + HALF, i * 128 : (i + 1) * 128] = piece[:, 0:128]
                out_ref[g, m * BLK + HALF : m * BLK + BLK, i * 128 : (i + 1) * 128] = piece[:, 128:256]
            return 0

        lax.fori_loop(0, ROWS, step, 0, unroll=True)


def fill_window(window, pieces):
    for o, piece in enumerate(pieces):
        for m in range(2):
            at = o * ROWS * BLK
            window[m, at : at + ROWS * BLK, :] = piece[m].reshape(ROWS * BLK, WIDE)


def rights(window, where_ref, same_ref, other_ref, g):
    stacks = ([], [])
    for a in range(SLOTS):
        i = g * SLOTS + a
        at = pl.multiple_of(where_ref[0, i] * BLK, BLK)
        same = jnp.concatenate([same_ref[i]] * 4, axis=0)
        other = jnp.concatenate([other_ref[i]] * 4, axis=0)
        for m in range(2):
            blocks = window[m, pl.ds(at, BLK), :]
            stacks[m].append(jnp.concatenate([blocks * same, blocks * other], axis=1))
    return [jnp.concatenate(stack, axis=0) for stack in stacks]


def settle(product):
    return product[:, 0:WIDE] + pltpu.roll(product[:, WIDE:], WIDE // 2, 1)


def first_body(where_ref, same_ref, other_ref, x0, x1, x2, x3, x4, left_ref, pair_ref, mixed_ref, window):
    fill_window(window, (x0, x1, x2, x3, x4))

    def step(g, _):
        ground, response = rights(window, where_ref, same_ref, other_ref, g)
        product = jnp.dot(left_ref[g], ground, preferred_element_type=F32)
        crossed = jnp.dot(left_ref[g, BLK:], response, preferred_element_type=F32)
        mixed = settle(product[0:BLK] + crossed)
        mixed_ref[g] = mixed
        pair_ref[0, g] = settle(product[BLK:]).astype(BF16)
        pair_ref[1, g] = mixed.astype(BF16)
        return 0

    lax.fori_loop(0, ROWS, step, 0, unroll=True)


def second_body(where_ref, same_ref, other_ref, x0, x1, x2, x3, x4, left_ref, mixed_ref, out_ref, window):
    fill_window(window, (x0, x1, x2, x3, x4))

    def step(g, _):
        square, mixed = rights(window, where_ref, same_ref, other_ref, g)
        cubic = jnp.dot(left_ref[g, 0:BLK], square, preferred_element_type=F32)
        cubic = settle(cubic + jnp.dot(left_ref[g, BLK:], mixed, preferred_element_type=F32))
        out_ref[g] = (3.0 * mixed_ref[g] - 2.0 * cubic).astype(BF16)
        return 0

    lax.fori_loop(0, ROWS, step, 0, unroll=True)


def join_body(in_ref, out_ref, turned):
    for r in range(ROWS):
        first, second = in_ref[r, 0:HALF].astype(F32), in_ref[r, HALF:BLK].astype(F32)
        for i, lines in enumerate(cross(first, second)):
            turned[pl.ds((K8 * r + i) * TILES, TILES), :] = lines
    for t in range(TILES):
        out_ref[0, :, t * 128 : (t + 1) * 128] = turned[pl.ds(t, SLOTS, stride=TILES), :].astype(BF16)


def partner(column, distance, shifted):
    size = NB // ROWS
    back = distance if shifted else 0
    return (((column - back) % size ^ distance) + back) % size


def trade(block, distance, shifted):
    columns, rows = lax.axis_size("col"), lax.axis_size("row")
    route = []
    for c in range(columns):
        for r in range(rows):
            route.append((c * rows + r, partner(c, distance, shifted != (r % 2 == 1)) * rows + r))
    return lax.ppermute(block, ("col", "row"), route)


def surround(block):
    turns = ((1, False), (1, True), (2, True), (2, False))
    return [trade(block, distance, shifted) for distance, shifted in turns] + [block]


def local(ground, response, pattern):
    rows = jax.ShapeDtypeStruct((2, ROWS, BLK, WIDE), BF16)
    mask = jax.ShapeDtypeStruct((ROWS * SLOTS, 16, WIDE), BF16)
    smem = pl.BlockSpec(memory_space=pltpu.SMEM)
    turned = pltpu.VMEM((SLOTS * TILES, 128), F32)
    held = pltpu.VMEM((2, ROWS, SLOTS, BLK * BLK), BF16)
    window = pltpu.VMEM((2, 5 * ROWS * BLK, WIDE), BF16)
    ground, response = (pltpu.with_memory_space_constraint(x, pltpu.HBM) for x in (ground, response))
    cut = call(
        slice_body,
        "slice",
        rows,
        [
            held,
            pltpu.VMEM((2, 2, ROWS * HALF, 128), F32),
            pltpu.SemaphoreType.DMA((2,)),
        ],
        [pl.BlockSpec(memory_space=pltpu.HBM)] * 2,
        2 * 2 * 16 * 128 * 4096,
        5 << 20,
        SLICE_BYTES,
    )(ground, response)
    cut, ground, response, pattern = lax.optimization_barrier((cut, ground, response, pattern))
    pieces = surround(cut)
    groups = jnp.where(pattern < 0, -1, pattern // ROWS).T
    left, place, same, other = call(
        left_body,
        "left",
        (jax.ShapeDtypeStruct((ROWS, 2 * BLK, SLOTS * BLK), BF16), jax.ShapeDtypeStruct((1, WIDE), jnp.int32), mask, mask),
        [turned, held, pltpu.SemaphoreType.DMA((2,))],
        in_vmem(1) + [pl.BlockSpec(memory_space=pltpu.HBM)] * 2,
        2 * 4096 * 256 * 256,
        5 << 20,
    )(groups, ground, response)
    flops = 2 * ROWS * BLK * 1024 * 128
    pair, mixed = call(
        first_body,
        "first",
        (rows, jax.ShapeDtypeStruct((ROWS, BLK, WIDE), F32)),
        [window],
        [smem] + in_vmem(8),
        3 * flops,
        5 << 20,
    )(place, same, other, *pieces, left)
    pieces = surround(pair)
    part = call(
        second_body,
        "second",
        jax.ShapeDtypeStruct((ROWS, BLK, WIDE), BF16),
        [window],
        [smem] + in_vmem(9),
        2 * flops,
        5 << 20,
    )(place, same, other, *pieces, left, mixed)
    part = lax.all_to_all(part, "row", 0, 0, tiled=True)
    return call(
        join_body,
        "join",
        jax.ShapeDtypeStruct((1, SLOTS, BLK * BLK), BF16),
        [turned],
        in_vmem(1),
        0,
        1 << 18,
    )(part)


def solution(mesh):
    in_specs = (P("col", None, None), P("col", None, None), P())
    out_specs = P(("col", "row"), None, None)
    return jax.shard_map(local, mesh=mesh, in_specs=in_specs, out_specs=out_specs, check_vma=False)
```

```python
import jax
import jax.numpy as jnp
from jax import lax
from jax.experimental import pallas as pl
from jax.experimental.pallas import tpu as pltpu
from jax.sharding import PartitionSpec as P

BLK = 64
K8 = 2
REACH = 2
NB = 512
SLOTS = 16
ROWS = 8
WIDE = K8 * BLK
TILES = BLK * BLK // 128
HALF = TILES
F32, BF16 = jnp.float32, jnp.bfloat16
VMEM_BYTES = 16 * 1024 * 1024


SLICE_BYTES = 8 * 1024 * 1024


def call(body, name, out_shape, scratch, in_specs, flops, moved, vmem=VMEM_BYTES):
    del name
    return pl.pallas_call(
        body,
        out_shape=out_shape,
        in_specs=in_specs,
        out_specs=jax.tree.map(lambda _: pl.BlockSpec(memory_space=pltpu.VMEM), out_shape),
        scratch_shapes=scratch,
        compiler_params=pltpu.CompilerParams(vmem_limit_bytes=vmem),
        cost_estimate=pl.CostEstimate(flops=flops, bytes_accessed=moved, transcendentals=0),
    )


def in_vmem(count):
    return [pl.BlockSpec(memory_space=pltpu.VMEM)] * count


def by_slot(rows_ref, g, turned):
    flat = rows_ref[g]
    for t in range(TILES):
        turned[pl.ds(t * SLOTS, SLOTS), :] = flat[:, t * 128 : (t + 1) * 128].astype(F32)
    return [turned[pl.ds(b, TILES, stride=SLOTS), :].astype(BF16) for b in range(SLOTS)]


def cross(a, b):
    low = lax.broadcasted_iota(jnp.int32, a.shape, 1) < BLK
    return jnp.where(low, a, pltpu.roll(b, BLK, 1)), jnp.where(low, pltpu.roll(a, BLK, 1), b)


def fetch(sources, held, arrived):
    copies = [pltpu.make_async_copy(source, held.at[m], arrived.at[m]) for m, source in enumerate(sources)]
    for copy in copies:
        copy.start()
    return copies


def slice_body(ground_hbm, response_hbm, out_ref, held, placed, arrived):
    copies = fetch((ground_hbm, response_hbm), held, arrived)
    line = lax.broadcasted_iota(jnp.int32, (K8 * ROWS, ROWS * SLOTS), 0)
    slot = lax.broadcasted_iota(jnp.int32, (K8 * ROWS, ROWS * SLOTS), 1)
    want = line % ROWS * SLOTS + K8 * lax.axis_index("row") + line // ROWS
    pick = jnp.where(slot == want, 1.0, 0.0).astype(BF16)
    for m in range(2):
        copies[m].wait()
        flat = held[m].reshape(ROWS * SLOTS, BLK * BLK)
        mine = jnp.dot(pick, flat, preferred_element_type=F32)
        for t in range(TILES):
            part = mine[:, t * 128 : (t + 1) * 128]
            for half, lines in enumerate(cross(part[0:ROWS], part[ROWS:])):
                placed[m, half, pl.ds(t, ROWS, stride=HALF), :] = lines
        for half in range(2):
            lines = placed[m, half].astype(BF16).reshape(ROWS, HALF, 128)
            out_ref[m, :, half * HALF : (half + 1) * HALF, :] = lines


def lookup(groups_ref, place_ref, same_ref, other_ref):
    column, odd = lax.axis_index("col"), lax.axis_index("row") % 2
    groups = groups_ref[...].astype(F32).astype(BF16)
    line = lax.broadcasted_iota(jnp.int32, (NB, WIDE), 0)
    lane = lax.broadcasted_iota(jnp.int32, (NB, WIDE), 1)
    mine = jnp.where(line == column * ROWS + lane // SLOTS, 1.0, 0.0).astype(BF16)
    near = jnp.dot(groups, mine, preferred_element_type=F32)
    slot = lax.broadcasted_iota(jnp.int32, (SLOTS, WIDE), 0)
    pair = lax.broadcasted_iota(jnp.int32, (SLOTS, WIDE), 1)
    home = jnp.sum(jnp.where(slot == pair % SLOTS, near, 0.0), axis=0, keepdims=True)
    live = home >= 0.0
    group = jnp.where(live, home, 0.0).astype(jnp.int32)
    kind = pair[0:1] % SLOTS // K8
    behind = column - group
    size = NB // ROWS
    behind = jnp.where(behind > REACH, behind - size, jnp.where(behind < -REACH, behind + size, behind))
    ahead = jnp.where(behind < 0, 1, 0)
    twice = jnp.where(behind > 1, 1, jnp.where(behind < -1, 1, 0))
    low = twice * (1 - column % 4 // 2) + (1 - twice) * (1 - column % 2)
    plain = 1 - jnp.abs(ahead - low)
    piece = jnp.where(behind == 0, 4, twice + 2 * (plain + odd * (1 - 2 * plain)))
    place_ref[...] = jnp.where(live, piece, 4) * ROWS + kind
    theirs = jnp.where(line == group * ROWS + kind, 1.0, 0.0).astype(BF16)
    far = jnp.dot(groups, theirs, preferred_element_type=F32)
    i = lax.broadcasted_iota(jnp.int32, (SLOTS, SLOTS), 0)
    j = lax.broadcasted_iota(jnp.int32, (SLOTS, SLOTS), 1)
    swap = jnp.where(i // K8 * K8 + 1 - i % K8 == j, 1.0, 0.0).astype(BF16)
    spread = jnp.where(slot == K8 * lax.axis_index("row") + pair // BLK, 1.0, 0.0).astype(BF16)
    facing = jnp.dot(swap, near.astype(BF16), preferred_element_type=F32)
    for ours, out_ref in ((near, same_ref), (facing, other_ref)):
        hit = jnp.where((far == ours) & (ours >= 0.0) & live, 1.0, 0.0).astype(BF16)
        mask = lax.dot_general(hit, spread, (((0,), (0,)), ((), ())), preferred_element_type=F32)
        for n in range(ROWS * SLOTS):
            out_ref[n] = jnp.broadcast_to(mask[n : n + 1], (16, WIDE)).astype(BF16)


def left_body(groups_ref, ground_hbm, response_hbm, out_ref, place_ref, same_ref, other_ref, turned, held, arrived):
    copies = fetch((response_hbm, ground_hbm), held, arrived)
    lookup(groups_ref, place_ref, same_ref, other_ref)
    src = lax.broadcasted_iota(jnp.int32, (256, 256), 0)
    dst = lax.broadcasted_iota(jnp.int32, (256, 256), 1)
    two, half, col = src // 128, src // BLK % 2, src % BLK
    want = half * 128 + two * BLK + (col % 2) * HALF + col // 2
    turn = jnp.where(dst == want, 1.0, 0.0).astype(BF16)
    for m in range(2):
        copies[m].wait()

        def step(g, _, m=m):
            parts = by_slot(held.at[m], g, turned)
            pairs = [jnp.concatenate(parts[b : b + 2], axis=1) for b in range(0, SLOTS, 2)]
            both = jnp.dot(jnp.concatenate(pairs, axis=0), turn, preferred_element_type=F32).astype(BF16)
            for i in range(SLOTS // 2):
                piece = both[i * TILES : (i + 1) * TILES]
                out_ref[g, m * BLK : m * BLK + HALF, i * 128 : (i + 1) * 128] = piece[:, 0:128]
                out_ref[g, m * BLK + HALF : m * BLK + BLK, i * 128 : (i + 1) * 128] = piece[:, 128:256]
            return 0

        lax.fori_loop(0, ROWS, step, 0, unroll=True)


def fill_window(window, pieces):
    for o, piece in enumerate(pieces):
        for m in range(2):
            at = o * ROWS * BLK
            window[m, at : at + ROWS * BLK, :] = piece[m].reshape(ROWS * BLK, WIDE)


def rights(window, where_ref, same_ref, other_ref, g):
    stacks = ([], [])
    for a in range(SLOTS):
        i = g * SLOTS + a
        at = pl.multiple_of(where_ref[0, i] * BLK, BLK)
        same = jnp.concatenate([same_ref[i]] * 4, axis=0)
        other = jnp.concatenate([other_ref[i]] * 4, axis=0)
        for m in range(2):
            blocks = window[m, pl.ds(at, BLK), :]
            stacks[m].append(jnp.concatenate([blocks * same, blocks * other], axis=1))
    return [jnp.concatenate(stack, axis=0) for stack in stacks]


def settle(product):
    return product[:, 0:WIDE] + pltpu.roll(product[:, WIDE:], WIDE // 2, 1)


def first_body(where_ref, same_ref, other_ref, x0, x1, x2, x3, x4, left_ref, pair_ref, mixed_ref, window):
    fill_window(window, (x0, x1, x2, x3, x4))

    def step(g, _):
        ground, response = rights(window, where_ref, same_ref, other_ref, g)
        product = jnp.dot(left_ref[g], ground, preferred_element_type=F32)
        crossed = jnp.dot(left_ref[g, BLK:], response, preferred_element_type=F32)
        mixed = settle(product[0:BLK] + crossed)
        mixed_ref[g] = mixed
        pair_ref[0, g] = settle(product[BLK:]).astype(BF16)
        pair_ref[1, g] = mixed.astype(BF16)
        return 0

    lax.fori_loop(0, ROWS, step, 0, unroll=True)


def second_body(where_ref, same_ref, other_ref, x0, x1, x2, x3, x4, left_ref, mixed_ref, out_ref, window):
    fill_window(window, (x0, x1, x2, x3, x4))

    def step(g, _):
        square, mixed = rights(window, where_ref, same_ref, other_ref, g)
        cubic = jnp.dot(left_ref[g, 0:BLK], square, preferred_element_type=F32)
        cubic = settle(cubic + jnp.dot(left_ref[g, BLK:], mixed, preferred_element_type=F32))
        out_ref[g] = (3.0 * mixed_ref[g] - 2.0 * cubic).astype(BF16)
        return 0

    lax.fori_loop(0, ROWS, step, 0, unroll=True)


def join_body(in_ref, out_ref, turned):
    for r in range(ROWS):
        first, second = in_ref[r, 0:HALF].astype(F32), in_ref[r, HALF:BLK].astype(F32)
        for i, lines in enumerate(cross(first, second)):
            turned[pl.ds((K8 * r + i) * TILES, TILES), :] = lines
    for t in range(TILES):
        out_ref[0, :, t * 128 : (t + 1) * 128] = turned[pl.ds(t, SLOTS, stride=TILES), :].astype(BF16)


def partner(column, distance, shifted):
    size = NB // ROWS
    back = distance if shifted else 0
    return (((column - back) % size ^ distance) + back) % size


def trade(block, distance, shifted):
    columns, rows = lax.axis_size("col"), lax.axis_size("row")
    route = []
    for c in range(columns):
        for r in range(rows):
            route.append((c * rows + r, partner(c, distance, shifted != (r % 2 == 1)) * rows + r))
    return lax.ppermute(block, ("col", "row"), route)


def surround(block):
    return [trade(block, distance, shifted) for shifted in (True, False) for distance in (1, 2)] + [block]


def local(ground, response, pattern):
    rows = jax.ShapeDtypeStruct((2, ROWS, BLK, WIDE), BF16)
    mask = jax.ShapeDtypeStruct((ROWS * SLOTS, 16, WIDE), BF16)
    smem = pl.BlockSpec(memory_space=pltpu.SMEM)
    turned = pltpu.VMEM((SLOTS * TILES, 128), F32)
    held = pltpu.VMEM((2, ROWS, SLOTS, BLK * BLK), BF16)
    window = pltpu.VMEM((2, 5 * ROWS * BLK, WIDE), BF16)
    ground, response = (pltpu.with_memory_space_constraint(x, pltpu.HBM) for x in (ground, response))
    cut = call(
        slice_body,
        "slice",
        rows,
        [
            held,
            pltpu.VMEM((2, 2, ROWS * HALF, 128), F32),
            pltpu.SemaphoreType.DMA((2,)),
        ],
        [pl.BlockSpec(memory_space=pltpu.HBM)] * 2,
        2 * 2 * 16 * 128 * 4096,
        5 << 20,
        SLICE_BYTES,
    )(ground, response)
    cut, ground, response, pattern = lax.optimization_barrier((cut, ground, response, pattern))
    pieces = surround(cut)
    groups = jnp.where(pattern < 0, -1, pattern // ROWS).T
    left, place, same, other = call(
        left_body,
        "left",
        (jax.ShapeDtypeStruct((ROWS, 2 * BLK, SLOTS * BLK), BF16), jax.ShapeDtypeStruct((1, WIDE), jnp.int32), mask, mask),
        [turned, held, pltpu.SemaphoreType.DMA((2,))],
        in_vmem(1) + [pl.BlockSpec(memory_space=pltpu.HBM)] * 2,
        2 * 4096 * 256 * 256,
        5 << 20,
    )(groups, ground, response)
    flops = 2 * ROWS * BLK * 1024 * 128
    pair, mixed = call(
        first_body,
        "first",
        (rows, jax.ShapeDtypeStruct((ROWS, BLK, WIDE), F32)),
        [window],
        [smem] + in_vmem(8),
        3 * flops,
        5 << 20,
    )(place, same, other, *pieces, left)
    pieces = surround(pair)
    part = call(
        second_body,
        "second",
        jax.ShapeDtypeStruct((ROWS, BLK, WIDE), BF16),
        [window],
        [smem] + in_vmem(9),
        2 * flops,
        5 << 20,
    )(place, same, other, *pieces, left, mixed)
    part = lax.all_to_all(part, "row", 0, 0, tiled=True)
    return call(
        join_body,
        "join",
        jax.ShapeDtypeStruct((1, SLOTS, BLK * BLK), BF16),
        [turned],
        in_vmem(1),
        0,
        1 << 18,
    )(part)


def solution(mesh):
    in_specs = (P("col", None, None), P("col", None, None), P())
    out_specs = P(("col", "row"), None, None)
    return jax.shard_map(local, mesh=mesh, in_specs=in_specs, out_specs=out_specs, check_vma=False)
```
